32 devices in a mesh: seq: 4 (over y, core), head: 4 (over z), rep: 2 (over x).
Axes of the slice: x: 2, y: 2, z: 4, core: 2. Of those that a mesh axis runs over, the one named last changes fastest.
Arguments:
- queries: bfloat16 [2048, 3072], P(('seq', 'rep'), 'head'), may hold values from -190 to 190
- keys: bfloat16 [2048, 3072], P(('seq', 'rep'), 'head'), may hold values from -6 to 6
- values: bfloat16 [2048, 3072], P(('seq', 'rep'), 'head'), may hold values from -6 to 6
- grad_output: bfloat16 [2048, 3072], P(('seq', 'rep'), 'head'), may hold values from -12 to 12
- out_weight: bfloat16 [3072, 3072], P('head'), may hold values from -0.109375 to 0.109375
- text_keys: bfloat16 [256, 3072], P(None, 'head'), may hold values from -7 to 7
- text_values: bfloat16 [256, 3072], P(None, 'head'), may hold values from -6 to 6
- mask_lists: int32 [16, 3], replicated, may hold values from 0 to 15, as said below
- text_owner: int32 [256], replicated, may hold values from 0 to 7, as said below
Outputs:
- query_grads: bfloat16 [2048, 3072], P(('seq', 'rep'), 'head')
- key_grads: bfloat16 [2048, 3072], P(('seq', 'rep'), 'head')
- value_grads: bfloat16 [2048, 3072], P(('seq', 'rep'), 'head')
- text_key_grads: bfloat16 [512, 3072], P(('seq', 'rep'), 'head')
- text_value_grads: bfloat16 [512, 3072], P(('seq', 'rep'), 'head')
The draws below stay inside these ranges and needn't reach their ends.
Inputs may be any that keep to these rules, and one draw needn't show every extreme that they name: Video tokens s * 256 to (s + 1) * 256 - 1 form slab s. Row t of mask_lists begins with t itself; its other 2 entries are distinct existing tiles other than t of the slabs t // 2 - 1, t // 2 and t // 2 + 1. `text_owner`: no slab owns more than 64 text tokens, and some slab owns exactly 64.
All inputs are finite; a program needn't handle non-finite values.
Results may differ from the reference program's by a relative error of at most 0.0156.
Values may be sent and summed in bfloat16 or wider, within the bound.
No kernel may reach another device: no remote copies, remote signals or barrier semaphores. Data moves between devices by JAX's collectives and lax.ppermute only.
A program may use at most 64 MiB of HBM per device.

```python
import jax
import jax.numpy as jnp
from jax import lax

D = 3072
HEADS = 24
HD = 128
FRAME = 256
TILE = 128
KB = 3
TEXT = 256
FRAMES = 8
VIDEO = 2048
QTILES = 16
CAP = 64
SLOTS = 512
HH = 3072


def shared_floats(key):
    base = jax.random.fold_in(key, 5)
    key_q, key_t = jax.random.split(base, 2)
    queries = jnp.clip(jax.random.normal(key_q, (VIDEO, HEADS * HD), jnp.float32), -6.0, 6.0)
    text = jnp.clip(jax.random.normal(key_t, (TEXT, HEADS * HD), jnp.float32), -6.0, 6.0)
    return (queries, text)


def draw_queries(key, part):
    return shared_floats(key)[0].astype(jnp.bfloat16)


def draw_text_keys(key, part):
    return shared_floats(key)[1].astype(jnp.bfloat16)


def draw_mask_lists(key, part):
    per_slab = FRAME // TILE
    tiles = jnp.arange(QTILES, dtype=jnp.int32)
    first = (tiles // per_slab - 1) * per_slab
    offsets = jnp.arange(3 * per_slab, dtype=jnp.int32)
    candidates = first[:, None] + offsets[None, :]
    usable = (candidates >= 0) & (candidates < QTILES) & (candidates != tiles[:, None])
    random_part = jax.random.randint(jax.random.fold_in(key, 17), (QTILES, 3 * per_slab), 0, 1 << 20)
    ranking = jnp.where(usable, random_part * (3 * per_slab) + offsets[None, :], -1 - offsets[None, :])
    unused, picks = lax.top_k(ranking, KB - 1)
    chosen = jnp.take_along_axis(candidates, picks, axis=1)
    return jnp.concatenate([tiles[:, None], chosen], axis=1).astype(jnp.int32)


def draw_text_owner(key, part):
    key_f, key_o, key_s = jax.random.split(jax.random.fold_in(key, 11), 3)
    busiest = jax.random.randint(key_f, (), 0, FRAMES)
    placing = jax.random.permutation(key_o, TEXT)
    others = jax.random.permutation(key_s, (FRAMES - 1) * CAP)[:TEXT - CAP] // CAP
    others = (others + (others >= busiest).astype(jnp.int32)).astype(jnp.int32)
    assigned = jnp.concatenate([jnp.full((CAP,), busiest, jnp.int32), others])
    return jnp.zeros((TEXT,), jnp.int32).at[placing].set(assigned)


def steps_of(stream_key, shape, cuts, low, largest):
    level = 1.0
    for axis_at, shards_of in cuts:
        draws = jax.random.uniform(jax.random.fold_in(jax.random.fold_in(stream_key, 6), axis_at), (shards_of,), jnp.float32, low / len(cuts), largest / len(cuts))
        level = level * jnp.repeat(jnp.exp(draws), shape[axis_at] // shards_of).reshape((-1,) + (1,) * (len(shape) - 1 - axis_at))
    return level


def scatter_about(stream_key, dims, scale, most, pieces=(), held_as=jnp.bfloat16):
    values = scale * jax.random.normal(stream_key, dims, jnp.float32)
    if pieces:
        values = values * steps_of(stream_key, dims, pieces, -0.22, 0.18)
    return jnp.clip(values, -most, most).astype(held_as)


def setup_inputs(seed: int = 0) -> dict:
    arg_keys = jax.random.split(jax.random.key(seed), 10)
    return {
        "queries": draw_queries(jax.random.fold_in(arg_keys[9], 71), 0),
        "keys": scatter_about(arg_keys[1], (VIDEO, HH), 1.0, 6.0, ((0, 8), (1, 4))),
        "values": scatter_about(arg_keys[2], (VIDEO, HH), 1.0, 6.0, ((0, 8), (1, 4))),
        "grad_output": scatter_about(arg_keys[3], (VIDEO, D), 2.0, 12.0, ((0, 8), (1, 4))),
        "out_weight": scatter_about(arg_keys[4], (HH, D), D ** -0.5, 0.109375, ((0, 4),)),
        "text_keys": draw_text_keys(jax.random.fold_in(arg_keys[9], 71), 0),
        "text_values": scatter_about(arg_keys[6], (TEXT, HH), 1.0, 6.0, ((1, 4),)),
        "mask_lists": draw_mask_lists(jax.random.fold_in(arg_keys[9], 71), 0),
        "text_owner": draw_text_owner(jax.random.fold_in(arg_keys[9], 71), 0),
    }


def reference(queries, keys, values, grad_output, out_weight, text_keys, text_values, mask_lists, text_owner):
    scale = HD ** -0.5
    grad_heads = jnp.dot(grad_output, out_weight.T, preferred_element_type=jnp.float32).astype(jnp.bfloat16)
    q_all = queries.reshape(VIDEO, HEADS, HD)
    k_all = keys.reshape(VIDEO, HEADS, HD)
    v_all = values.reshape(VIDEO, HEADS, HD)
    g_all = grad_heads.reshape(VIDEO, HEADS, HD)
    text_k = text_keys.reshape(TEXT, HEADS, HD).astype(jnp.float32)
    text_v = text_values.reshape(TEXT, HEADS, HD).astype(jnp.float32)
    within = jnp.arange(TILE, dtype=jnp.int32)
    video_n = KB * TILE

    def step(carry, tile):
        key_acc, value_acc, tkey_acc, tvalue_acc = carry
        start = (tile * TILE).astype(jnp.int32)
        q_tile = lax.dynamic_slice_in_dim(q_all, start, TILE, 0).astype(jnp.float32)
        g_tile = lax.dynamic_slice_in_dim(g_all, start, TILE, 0).astype(jnp.float32)
        listed = lax.dynamic_index_in_dim(mask_lists, tile, 0, keepdims=False)
        index = (listed[:, None] * TILE + within[None, :]).reshape(-1).astype(jnp.int32)
        k_tile = jnp.concatenate([k_all[index].astype(jnp.float32), text_k], axis=0)
        v_tile = jnp.concatenate([v_all[index].astype(jnp.float32), text_v], axis=0)
        scores = scale * jnp.einsum("qhe,khe->hqk", q_tile, k_tile)
        top = jnp.max(scores, axis=2, keepdims=True)
        lse = top + jnp.log(jnp.sum(jnp.exp(scores - top), axis=2, keepdims=True))
        prob = jnp.exp(scores - lse)
        prob_half = lax.optimization_barrier(prob.astype(jnp.bfloat16)).astype(jnp.float32)
        attended = jnp.einsum("hqk,khe->qhe", prob_half, v_tile)
        delta = jnp.einsum("qhe,qhe->hq", g_tile, attended)[:, :, None]
        dprob = jnp.einsum("qhe,khe->hqk", g_tile, v_tile)
        dscore = lax.optimization_barrier((prob * (dprob - delta)).astype(jnp.bfloat16)).astype(jnp.float32)
        dq = (scale * jnp.einsum("hqk,khe->qhe", dscore, k_tile)).astype(jnp.bfloat16)
        dk = scale * jnp.einsum("hqk,qhe->khe", dscore, q_tile)
        dv = jnp.einsum("hqk,qhe->khe", prob_half, g_tile)
        key_acc = key_acc.at[index].add(dk[:video_n])
        value_acc = value_acc.at[index].add(dv[:video_n])
        tkey_acc = tkey_acc + dk[video_n:]
        tvalue_acc = tvalue_acc + dv[video_n:]
        return (key_acc, value_acc, tkey_acc, tvalue_acc), dq

    start_carry = (jnp.zeros((VIDEO, HEADS, HD), jnp.float32), jnp.zeros((VIDEO, HEADS, HD), jnp.float32),
                   jnp.zeros((TEXT, HEADS, HD), jnp.float32), jnp.zeros((TEXT, HEADS, HD), jnp.float32))
    carry, dq_tiles = lax.scan(step, start_carry, jnp.arange(QTILES, dtype=jnp.int32))
    key_acc, value_acc, tkey_acc, tvalue_acc = carry
    query_grads = dq_tiles.reshape(VIDEO, HEADS * HD)
    key_grads = key_acc.reshape(VIDEO, HEADS * HD).astype(jnp.bfloat16)
    value_grads = value_acc.reshape(VIDEO, HEADS * HD).astype(jnp.bfloat16)
    owner_hot = (text_owner[:, None] == jnp.arange(FRAMES, dtype=jnp.int32)[None, :]).astype(jnp.int32)
    rank = jnp.sum(owner_hot * (jnp.cumsum(owner_hot, axis=0) - 1), axis=1).astype(jnp.int32)
    slot = (text_owner * CAP + rank).astype(jnp.int32)
    text_key_grads = jnp.zeros((SLOTS, HEADS * HD), jnp.bfloat16).at[slot].set(
        tkey_acc.reshape(TEXT, HEADS * HD).astype(jnp.bfloat16))
    text_value_grads = jnp.zeros((SLOTS, HEADS * HD), jnp.bfloat16).at[slot].set(
        tvalue_acc.reshape(TEXT, HEADS * HD).astype(jnp.bfloat16))
    return (query_grads, key_grads, value_grads, text_key_grads, text_value_grads)
```

```python
import functools
import math

import jax
import jax.numpy as jnp
from jax import lax
from jax.experimental import pallas as pl
from jax.experimental.pallas import tpu as pltpu
from jax.sharding import PartitionSpec as P

HD = 128
TILE = 128
AUX = 16
SCALE = HD ** (-0.5)
SCALE2 = SCALE * math.log2(math.e)
OFF = 1e30
BF = jnp.bfloat16
F32 = jnp.float32


def nt(a, b):
    return lax.dot_general(a, b, (((1,), (1,)), ((), ())), preferred_element_type=F32)


def nn(a, b):
    return lax.dot_general(a, b, (((1,), (0,)), ((), ())), preferred_element_type=F32)


def tn(a, b):
    return lax.dot_general(a, b, (((0,), (0,)), ((), ())), preferred_element_type=F32)


def lanes(h):
    return slice(h * HD, (h + 1) * HD)


def source_tile(place, lists, tile, entry):
    slab, mate = place[0], place[1]
    listed = lists[tile, entry]
    owner = lax.shift_right_logical(listed, 1)
    source = jnp.where(owner == slab, 0, jnp.where(owner == mate, 1, 2))
    return pl.multiple_of((source * 2 + (listed & 1)) * TILE, TILE)


def stack_tiles(parts, wide):
    frame = parts[0].shape[0]
    for i, part in enumerate(parts):
        wide[i * frame : (i + 1) * frame, :] = part[...]


def forward_kernel(
    place, lists, q, k0, k1, k2, v0, v1, v2, tk, tv, out, lse, wide_k, wide_v
):
    stack_tiles((k0, k1, k2), wide_k)
    stack_tiles((v0, v1, v2), wide_v)
    heads = q.shape[1] // HD
    for tile in range(q.shape[0] // TILE):
        starts = [source_tile(place, lists, place[0] * 2 + tile, e) for e in range(3)]
        rows = slice(tile * TILE, (tile + 1) * TILE)
        for h in range(heads):
            cols = lanes(h)
            keys = jnp.concatenate(
                [wide_k[pl.ds(a, TILE), cols] for a in starts] + [tk[:, cols]], axis=0
            )
            values = jnp.concatenate(
                [wide_v[pl.ds(a, TILE), cols] for a in starts] + [tv[:, cols]], axis=0
            )
            score = nt(keys, q[rows, cols])
            top = jnp.max(score, axis=0, keepdims=True)
            weight = jnp.exp2((score - top) * SCALE2)
            total = jnp.sum(weight, axis=0, keepdims=True)
            prob = (weight * (1.0 / total)).astype(BF)
            out[rows, cols] = tn(prob, values)
            lse[tile * 8 : (tile + 1) * 8, cols] = jnp.broadcast_to(
                top * SCALE2 + jnp.log2(total), (8, TILE)
            )


def split(x, count):
    parts = []
    for _ in range(count):
        head = x.astype(BF).astype(F32)
        parts.append(head)
        x = x - head
    return parts


def grad_kernel(chunk, n, place, *refs):
    parts, (weight, attended, lse, message) = refs[:n], refs[n:]
    rank = place[2]
    total = None
    depth = weight.shape[1] // n
    for step in range(n):
        source = lax.rem(rank - step + n, n)
        block = weight[:, pl.ds(pl.multiple_of(source * depth, 128), depth)]
        term = nt(parts[step][...], block)
        total = term if total is None else total + term
    half = total.astype(BF)
    message[:TILE, :] = half
    wide = half.astype(F32)
    row = lax.broadcasted_iota(jnp.int32, (AUX, TILE), 0)
    for h in range(half.shape[1] // HD):
        cols = lanes(h)
        product = wide[:, cols] * attended[chunk * TILE : (chunk + 1) * TILE, cols]
        delta = jnp.sum(product.T, axis=0, keepdims=True)
        extra = split(delta, 2) + split(lse[chunk * 8 : chunk * 8 + 1, cols], 3)
        block = jnp.zeros((AUX, TILE), F32)
        for i, line in enumerate(extra):
            block = jnp.where(row == i, jnp.broadcast_to(line, (AUX, TILE)), block)
        message[TILE : TILE + AUX, cols] = block.astype(BF)


def read_message(message, cols):
    g = message[:TILE, cols]
    aux = message[TILE : TILE + AUX, cols].astype(F32)
    delta = aux[0:1] + aux[1:2]
    lse = (aux[2:3] + aux[3:4]) + aux[4:5]
    return g, delta, lse


def query_kernel(
    place, lists, q, k0, k1, k2, v0, v1, v2, tk, tv, m0, m1, out, wide_k, wide_v
):
    stack_tiles((k0, k1, k2), wide_k)
    stack_tiles((v0, v1, v2), wide_v)
    heads = q.shape[1] // HD
    for tile, message in enumerate((m0, m1)):
        starts = [source_tile(place, lists, place[0] * 2 + tile, e) for e in range(3)]
        rows = slice(tile * TILE, (tile + 1) * TILE)
        for h in range(heads):
            cols = lanes(h)
            g, delta, lse = read_message(message, cols)
            keys = jnp.concatenate(
                [wide_k[pl.ds(a, TILE), cols] for a in starts] + [tk[:, cols]], axis=0
            )
            values = jnp.concatenate(
                [wide_v[pl.ds(a, TILE), cols] for a in starts] + [tv[:, cols]], axis=0
            )
            prob = jnp.exp2(nt(keys, q[rows, cols]) * SCALE2 - lse)
            dscore = (prob * (nt(values, g) - delta)).astype(BF)
            out[rows, cols] = (SCALE * tn(dscore, keys)).astype(BF)


def listed(place, lists, slab, tile, key_tile):
    count = lists.shape[0]
    query_tile = slab * 2 + tile
    row = jnp.clip(query_tile, 0, count - 1)
    wanted = place[0] * 2 + key_tile
    found = (lists[row, 0] == wanted) | (lists[row, 1] == wanted) | (lists[row, 2] == wanted)
    found = found & (query_tile >= 0) & (query_tile < count)
    return jnp.where(found, 0.0, OFF)


def key_terms(place, lists, slab, tile, keys, values, q, message, cols):
    g, delta, lse = read_message(message, cols)
    score = nt(keys, q) * SCALE2
    pieces = []
    for i in range(2):
        block = score[i * TILE : (i + 1) * TILE]
        pieces.append(block - (lse + listed(place, lists, slab, tile, i)))
    if keys.shape[0] > 2 * TILE:
        pieces.append(score[2 * TILE :] - lse)
    prob = jnp.exp2(jnp.concatenate(pieces, axis=0))
    dscore = (prob * (nt(values, g) - delta)).astype(BF)
    return nn(dscore, q), nn(prob.astype(BF), g)


def near_kernel(
    place, lists, k, v, sk, sv, valid, q0, q1, a0, a1, b0, b1,
    key_acc, value_acc, keep_k, keep_v, send_k, send_v,
):
    frame = k.shape[0]
    half = keep_k.shape[0]
    live = valid[...] > 0
    for h in range(k.shape[1] // HD):
        cols = lanes(h)
        keys = jnp.concatenate([k[:, cols], sk[:, cols]], axis=0)
        values = jnp.concatenate([v[:, cols], sv[:, cols]], axis=0)
        key_sum = value_sum = None
        for who, (q, messages) in enumerate(((q0, (a0, a1)), (q1, (b0, b1)))):
            for tile, message in enumerate(messages):
                rows = slice(tile * TILE, (tile + 1) * TILE)
                dk, dv = key_terms(
                    place, lists, place[who], tile, keys, values, q[rows, cols], message, cols
                )
                key_sum = dk if key_sum is None else key_sum + dk
                value_sum = dv if value_sum is None else value_sum + dv
        key_acc[:, cols] = key_sum[:frame]
        value_acc[:, cols] = value_sum[:frame]
        text_k = jnp.where(live, key_sum[frame:] * SCALE, 0.0)
        text_v = jnp.where(live, value_sum[frame:], 0.0)
        keep_k[:, cols] = text_k[:half]
        keep_v[:, cols] = text_v[:half]
        send_k[:, cols] = text_k[half:].astype(BF)
        send_v[:, cols] = text_v[half:].astype(BF)


def far_kernel(place, lists, k, v, q, m0, m1, key_acc, value_acc, key_out, value_out):
    for h in range(k.shape[1] // HD):
        cols = lanes(h)
        key_sum = key_acc[:, cols]
        value_sum = value_acc[:, cols]
        for tile, message in enumerate((m0, m1)):
            rows = slice(tile * TILE, (tile + 1) * TILE)
            dk, dv = key_terms(
                place, lists, place[3], tile, k[:, cols], v[:, cols], q[rows, cols], message, cols
            )
            key_sum = key_sum + dk
            value_sum = value_sum + dv
        key_out[:, cols] = (key_sum * SCALE).astype(BF)
        value_out[:, cols] = value_sum.astype(BF)


def call(kernel, name, outs, scalars, arrays, scratch=(), flops=0, size=0):
    return pl.pallas_call(
        kernel,
        name=name,
        out_shape=outs,
        in_specs=[pl.BlockSpec(memory_space=pltpu.SMEM)] * scalars
        + [pl.BlockSpec(memory_space=pltpu.VMEM)] * (len(arrays) - scalars),
        out_specs=jax.tree.map(lambda _: pl.BlockSpec(memory_space=pltpu.VMEM), outs),
        scratch_shapes=list(scratch),
        compiler_params=pltpu.CompilerParams(vmem_limit_bytes=48 << 20),
        cost_estimate=pl.CostEstimate(flops=flops, bytes_accessed=size, transcendentals=0),
    )(*arrays)


def local(
    queries, keys, values, grad_output, out_weight, text_keys, text_values, mask_lists, text_owner
):
    frame, width = queries.shape
    text_count = text_keys.shape[0]
    both = ("seq", "rep")
    seqs, reps, ranks = lax.axis_size("seq"), lax.axis_size("rep"), lax.axis_size("head")
    groups = seqs * reps
    slab = lax.axis_index(both)
    mate = slab ^ 1
    other = jnp.where(slab & 1, slab + 1, slab - 1)
    place = jnp.stack([slab, mate, lax.axis_index("head"), other]).astype(jnp.int32)

    def swap(x, distance=1):
        return lax.ppermute(x, both, [(i, i ^ distance) for i in range(groups)])

    def relay(x):
        def target(i):
            if i % 2 == 0:
                return i + 2 if i + 2 < groups else i + 1
            return i - 2 if i >= 2 else i - 1

        return lax.ppermute(x, both, [(i, target(i)) for i in range(groups)])

    def ring(x):
        return lax.ppermute(x, "head", [(i, (i + 1) % ranks) for i in range(ranks)])

    parts = [[grad_output[:TILE]], [grad_output[TILE:]]]
    for _ in range(ranks - 1):
        for chunk in parts:
            chunk.append(ring(chunk[-1]))

    mate_k, mate_v, mate_q = swap(keys), swap(values), swap(queries)
    far_k, far_v, far_q = relay(mate_k), relay(mate_v), relay(mate_q)

    capacity = 2 * text_count // groups
    slots = groups // 2 * capacity
    stages = []
    distance = 2
    while distance < groups:
        stages.append(distance)
        distance *= 2
    offsets = [0]
    for d in reversed(stages):
        offsets = offsets + [o ^ d for o in offsets]
    owners = slab ^ jnp.repeat(jnp.asarray(offsets, jnp.int32), capacity)
    wanted = owners * capacity + jnp.tile(jnp.arange(capacity, dtype=jnp.int32), len(offsets))
    token = jnp.arange(text_count, dtype=jnp.int32)
    same = (text_owner[:, None] == text_owner[None, :]) & (token[None, :] < token[:, None])
    slot = text_owner * capacity + jnp.sum(same.astype(jnp.int32), axis=1)
    placing = wanted[:, None] == slot[None, :]
    valid = jnp.broadcast_to(
        jnp.any(placing, axis=1, keepdims=True).astype(F32), (slots, HD)
    )
    placing = placing.astype(BF)
    slot_k = jnp.dot(placing, text_keys, preferred_element_type=BF)
    slot_v = jnp.dot(placing, text_values, preferred_element_type=BF)

    wide = pltpu.VMEM((3 * frame, width), BF)
    sds = jax.ShapeDtypeStruct
    attended, lse = call(
        forward_kernel,
        "attend",
        (sds((frame, width), F32), sds((16, width), F32)),
        2,
        (place, mask_lists, queries, keys, mate_k, far_k, values, mate_v, far_v, text_keys, text_values),
        (wide, wide),
        flops=2 * 2 * frame * 640 * width,
        size=5 << 20,
    )
    messages = [
        call(
            functools.partial(grad_kernel, i, ranks),
            f"grad_heads_{i}",
            sds((TILE + AUX, width), BF),
            1,
            (place, *parts[i], out_weight, attended, lse),
            flops=2 * TILE * width * out_weight.shape[1],
            size=7 << 20,
        )
        for i in range(2)
    ]
    mates = [swap(m) for m in messages]
    fars = [relay(m) for m in mates]
    query_grads = call(
        query_kernel,
        "query_grads",
        sds((frame, width), BF),
        2,
        (place, mask_lists, queries, keys, mate_k, far_k, values, mate_v, far_v, text_keys, text_values, *messages),
        (wide, wide),
        flops=3 * 2 * frame * 640 * width,
        size=5 << 20,
    )
    key_acc, value_acc, keep_k, keep_v, send_k, send_v = call(
        near_kernel,
        "near_keys",
        (sds((frame, width), F32),) * 2
        + (sds((slots // 2, width), F32),) * 2
        + (sds((slots // 2, width), BF),) * 2,
        2,
        (place, mask_lists, keys, values, slot_k, slot_v, valid, queries, mate_q, *messages, *mates),
        flops=4 * 2 * 512 * 512 * width,
        size=8 << 20,
    )
    key_grads, value_grads = call(
        far_kernel,
        "far_keys",
        (sds((frame, width), BF),) * 2,
        2,
        (place, mask_lists, keys, values, far_q, *fars, key_acc, value_acc),
        flops=4 * 2 * 256 * 256 * width,
        size=5 << 20,
    )
    keep = jnp.concatenate([keep_k, keep_v], axis=1)
    send = jnp.concatenate([send_k, send_v], axis=1)
    for i, d in enumerate(stages):
        total = keep + swap(send, d).astype(F32)
        if i + 1 < len(stages):
            rows = total.shape[0] // 2
            keep, send = total[:rows], total[rows:].astype(BF)
    total = total.astype(BF)
    return query_grads, key_grads, value_grads, total[:, :width], total[:, width:]


def solution(mesh):
    rows = P(("seq", "rep"), "head")
    return jax.shard_map(
        local,
        mesh=mesh,
        in_specs=(rows, rows, rows, rows, P("head", None), P(None, "head"), P(None, "head"), P(), P()),
        out_specs=(rows,) * 5,
        check_vma=False,
    )
```

```python
import functools
import math

import jax
import jax.numpy as jnp
from jax import lax
from jax.experimental import pallas as pl
from jax.experimental.pallas import tpu as pltpu
from jax.sharding import PartitionSpec as P

HD = 128
TILE = 128
AUX = 16
SCALE = HD ** (-0.5)
SCALE2 = SCALE * math.log2(math.e)
OFF = 1e30
BF = jnp.bfloat16
F32 = jnp.float32
LIMIT = 16 << 20


def nt(a, b):
    return lax.dot_general(a, b, (((1,), (1,)), ((), ())), preferred_element_type=F32)


def nn(a, b):
    return lax.dot_general(a, b, (((1,), (0,)), ((), ())), preferred_element_type=F32)


def tn(a, b):
    return lax.dot_general(a, b, (((0,), (0,)), ((), ())), preferred_element_type=F32)


def lanes(h):
    return slice(h * HD, (h + 1) * HD)


def source_tile(place, lists, tile, entry):
    slab, mate = place[0], place[1]
    listed = lists[tile, entry]
    owner = lax.shift_right_logical(listed, 1)
    source = jnp.where(owner == slab, 0, jnp.where(owner == mate, 1, 2))
    return pl.multiple_of((source * 2 + (listed & 1)) * TILE, TILE)


def stack_tiles(parts, wide):
    frame = parts[0].shape[0]
    for i, part in enumerate(parts):
        wide[i * frame : (i + 1) * frame, :] = part[...]


def slot_kernel(capacity, place, owner, tk, tv, sk, sv, valid):
    count = owner.shape[1]
    slots = sk.shape[0]
    across = jnp.broadcast_to(owner[...], (count, count))
    down = across.astype(F32).T.astype(jnp.int32)
    line = lax.broadcasted_iota(jnp.int32, (count, count), 0)
    lane = lax.broadcasted_iota(jnp.int32, (count, count), 1)
    rank = jnp.sum(
        jnp.where((across == down) & (line < lane), 1, 0), axis=0, keepdims=True
    )
    slot = owner[...] * capacity + rank
    row = lax.broadcasted_iota(jnp.int32, (slots, count), 0)
    group, inside = row // capacity, row % capacity
    bits = (slots // capacity).bit_length() - 1
    offset = jnp.zeros_like(row)
    for bit in range(bits):
        offset = offset + (((group >> (bits - 1 - bit)) & 1) << (bit + 1))
    wanted = (place[0] ^ offset) * capacity + inside
    chosen = jnp.where(wanted == jnp.broadcast_to(slot, (slots, count)), 1.0, 0.0)
    live = jnp.sum(chosen, axis=1, keepdims=True)
    chosen = chosen.astype(BF)
    sk[...] = nn(chosen, tk[...]).astype(BF)
    sv[...] = nn(chosen, tv[...]).astype(BF)
    valid[...] = jnp.broadcast_to(live, valid.shape)


def gathered(wide, text, starts, cols):
    return jnp.concatenate(
        [wide[pl.ds(a, TILE), cols] for a in starts] + [text[:, cols]], axis=0
    )


def split(x, count):
    parts = []
    for _ in range(count):
        head = x.astype(BF).astype(F32)
        parts.append(head)
        x = x - head
    return parts


def first_kernel(n, place, *refs):
    parts, weights, out = refs[: 2 * n], refs[2 * n : 3 * n], refs[3 * n]
    for chunk in range(2):
        total = None
        for part, weight in zip(parts[chunk * n : (chunk + 1) * n], weights):
            term = nt(part[...], weight[...])
            total = term if total is None else total + term
        out[chunk * TILE : (chunk + 1) * TILE, :] = total


def middle_kernel(place, a_before, a_last, b_before, first, w_before, w_last, out, partial):
    total = first[:TILE, :] + nt(a_before[...], w_before[...])
    out[...] = (total + nt(a_last[...], w_last[...])).astype(BF)
    partial[...] = first[TILE:, :] + nt(b_before[...], w_before[...])


def last_kernel(place, b_last, partial, w_last, out):
    out[...] = (partial[...] + nt(b_last[...], w_last[...])).astype(BF)


def softmax_kernel(
    place, lists, q, k0, k1, k2, v0, v1, v2, tk, tv, m0, m1, aux, dscores, wide_k, wide_v
):
    stack_tiles((k0, k1, k2), wide_k)
    stack_tiles((v0, v1, v2), wide_v)
    row = lax.broadcasted_iota(jnp.int32, (AUX, TILE), 0)
    size = dscores.shape[0] // 2
    for tile, message in enumerate((m0, m1)):
        starts = [source_tile(place, lists, place[0] * 2 + tile, e) for e in range(3)]
        rows = slice(tile * TILE, (tile + 1) * TILE)
        for h in range(q.shape[1] // HD):
            cols = lanes(h)
            score = nt(gathered(wide_k, tk, starts, cols), q[rows, cols])
            top = jnp.max(score, axis=0, keepdims=True)
            weight = jnp.exp2((score - top) * SCALE2)
            total = jnp.sum(weight, axis=0, keepdims=True)
            prob = weight * (1.0 / total)
            dprob = nt(gathered(wide_v, tv, starts, cols), message[:, cols])
            delta = jnp.sum(prob * dprob, axis=0, keepdims=True)
            dscores[tile * size : (tile + 1) * size, cols] = (prob * (dprob - delta)).astype(BF)
            lse = top * SCALE2 + jnp.log2(total)
            block = jnp.zeros((AUX, TILE), F32)
            for i, line in enumerate(split(delta, 2) + split(lse, 3)):
                block = jnp.where(row == i, jnp.broadcast_to(line, (AUX, TILE)), block)
            aux[tile * AUX : (tile + 1) * AUX, cols] = block.astype(BF)


def query_kernel(place, lists, k0, k1, k2, tk, dscores, out, wide_k):
    stack_tiles((k0, k1, k2), wide_k)
    size = dscores.shape[0] // 2
    for tile in range(2):
        starts = [source_tile(place, lists, place[0] * 2 + tile, e) for e in range(3)]
        rows = slice(tile * TILE, (tile + 1) * TILE)
        for h in range(out.shape[1] // HD):
            cols = lanes(h)
            dscore = dscores[tile * size : (tile + 1) * size, cols]
            keys = gathered(wide_k, tk, starts, cols)
            out[rows, cols] = (SCALE * tn(dscore, keys)).astype(BF)


def read_lines(aux, chunk, cols):
    lines = aux[chunk * AUX : (chunk + 1) * AUX, cols].astype(F32)
    return lines[0:1] + lines[1:2], (lines[2:3] + lines[3:4]) + lines[4:5]


def off_by(place, lists, slab, tile, key_tile):
    count = lists.shape[0]
    query_tile = slab * 2 + tile
    row = jnp.clip(query_tile, 0, count - 1)
    wanted = place[0] * 2 + key_tile
    found = (lists[row, 0] == wanted) | (lists[row, 1] == wanted) | (lists[row, 2] == wanted)
    found = found & (query_tile >= 0) & (query_tile < count)
    return jnp.where(found, 0.0, OFF)


def key_terms(offs, keys, values, q, m0, m1, aux, cols):
    lines = [read_lines(aux, i, cols) for i in range(2)]
    delta = jnp.concatenate([d for d, _ in lines], axis=1)
    lse = [l for _, l in lines]
    g = jnp.concatenate([m0[:, cols], m1[:, cols]], axis=0)
    score = nt(keys, q) * SCALE2
    pieces = []
    for i in range(2):
        line = jnp.concatenate([lse[t] + offs[t][i] for t in range(2)], axis=1)
        pieces.append(score[i * TILE : (i + 1) * TILE] - line)
    if keys.shape[0] > 2 * TILE:
        pieces.append(score[2 * TILE :] - jnp.concatenate(lse, axis=1))
    prob = jnp.exp2(jnp.concatenate(pieces, axis=0))
    dscore = (prob * (nt(values, g) - delta)).astype(BF)
    return nn(dscore, q), nn(prob.astype(BF), g)


def all_offs(place, lists, slab):
    return [[off_by(place, lists, slab, t, i) for i in range(2)] for t in range(2)]


def own_kernel(
    place, lists, k, v, sk, sv, q, m0, m1, aux, key_acc, value_acc, text_k, text_v
):
    frame = k.shape[0]
    offs = all_offs(place, lists, place[0])
    for h in range(k.shape[1] // HD):
        cols = lanes(h)
        keys = jnp.concatenate([k[:, cols], sk[:, cols]], axis=0)
        values = jnp.concatenate([v[:, cols], sv[:, cols]], axis=0)
        dk, dv = key_terms(offs, keys, values, q[:, cols], m0, m1, aux, cols)
        key_acc[:, cols] = dk[:frame]
        value_acc[:, cols] = dv[:frame]
        text_k[:, cols] = dk[frame:]
        text_v[:, cols] = dv[frame:]


def mate_kernel(
    place, lists, k, v, sk, sv, valid, q, m0, m1, aux, key_in, value_in, text_k, text_v,
    key_acc, value_acc, keep, send,
):
    frame, width = k.shape
    half = keep.shape[0]
    live = valid[...] > 0
    offs = all_offs(place, lists, place[1])
    for h in range(width // HD):
        cols = lanes(h)
        more = slice(width + h * HD, width + (h + 1) * HD)
        keys = jnp.concatenate([k[:, cols], sk[:, cols]], axis=0)
        values = jnp.concatenate([v[:, cols], sv[:, cols]], axis=0)
        dk, dv = key_terms(offs, keys, values, q[:, cols], m0, m1, aux, cols)
        key_acc[:, cols] = key_in[:, cols] + dk[:frame]
        value_acc[:, cols] = value_in[:, cols] + dv[:frame]
        part_k = jnp.where(live, (text_k[:, cols] + dk[frame:]) * SCALE, 0.0)
        part_v = jnp.where(live, text_v[:, cols] + dv[frame:], 0.0)
        keep[:, cols] = part_k[:half]
        keep[:, more] = part_v[:half]
        send[:, cols] = part_k[half:].astype(BF)
        send[:, more] = part_v[half:].astype(BF)


def far_kernel(place, lists, k, v, q, m0, m1, aux, key_acc, value_acc, key_out, value_out):
    offs = all_offs(place, lists, place[3])
    for h in range(k.shape[1] // HD):
        cols = lanes(h)
        dk, dv = key_terms(offs, k[:, cols], v[:, cols], q[:, cols], m0, m1, aux, cols)
        key_out[:, cols] = ((key_acc[:, cols] + dk) * SCALE).astype(BF)
        value_out[:, cols] = (value_acc[:, cols] + dv).astype(BF)


VMEM = pl.BlockSpec(memory_space=pltpu.VMEM)
SMEM = pl.BlockSpec(memory_space=pltpu.SMEM)


def call(kernel, name, outs, scalars, arrays, scratch=()):
    return pl.pallas_call(
        kernel,
        name=name,
        out_shape=outs,
        in_specs=[SMEM] * scalars + [VMEM] * (len(arrays) - scalars),
        out_specs=jax.tree.map(lambda _: VMEM, outs),
        scratch_shapes=list(scratch),
        compiler_params=pltpu.CompilerParams(vmem_limit_bytes=LIMIT),
    )(*arrays)


def call_blocks(kernel, name, outs, place, arrays, weight, steps):
    rows, depth = weight.shape[0], arrays[0].shape[1]
    ranks = weight.shape[1] // depth

    def block(step):
        return pl.BlockSpec(
            (rows, depth), lambda i, place: (0, lax.rem(place[2] - step + ranks, ranks))
        )

    return pl.pallas_call(
        kernel,
        name=name,
        out_shape=outs,
        grid_spec=pltpu.PrefetchScalarGridSpec(
            num_scalar_prefetch=1,
            grid=(1,),
            in_specs=[VMEM] * len(arrays) + [block(step) for step in steps],
            out_specs=jax.tree.map(lambda _: VMEM, outs),
        ),
        compiler_params=pltpu.CompilerParams(vmem_limit_bytes=LIMIT),
    )(place, *arrays, *([weight] * len(steps)))


def together(*arrays):
    return lax.optimization_barrier(arrays)


def local(
    queries, keys, values, grad_output, out_weight, text_keys, text_values, mask_lists, text_owner
):
    frame, width = queries.shape
    text_count = text_keys.shape[0]
    both = ("seq", "rep")
    seqs, reps, ranks = lax.axis_size("seq"), lax.axis_size("rep"), lax.axis_size("head")
    groups = seqs * reps
    slab = lax.axis_index(both)
    mate = slab ^ 1
    other = jnp.where(slab & 1, slab + 1, slab - 1)
    place = jnp.stack([slab, mate, lax.axis_index("head"), other]).astype(jnp.int32)

    def swap(x, distance=1):
        return lax.ppermute(x, both, [(i, i ^ distance) for i in range(groups)])

    def relay(x):
        def target(i):
            if i % 2 == 0:
                return i + 2 if i + 2 < groups else i + 1
            return i - 2 if i >= 2 else i - 1

        return lax.ppermute(x, both, [(i, target(i)) for i in range(groups)])

    def ring(x):
        return lax.ppermute(x, "head", [(i, (i + 1) % ranks) for i in range(ranks)])

    capacity = 2 * text_count // groups
    slots = groups // 2 * capacity
    sds = jax.ShapeDtypeStruct
    sk, sv, valid = call(
        functools.partial(slot_kernel, capacity),
        "slots",
        (sds((slots, width), BF),) * 2 + (sds((slots, HD), F32),),
        1,
        (place, text_owner.reshape(1, text_count), text_keys, text_values),
    )
    part_a, part_b = [grad_output[:TILE]], [grad_output[TILE:]]
    part_a.append(ring(part_a[0]))
    part_b.append(ring(part_b[0]))
    mate_v = swap(values)
    late_k, part_a[1] = together(keys, part_a[1])
    mate_k = swap(late_k)
    for _ in range(ranks - 2):
        part_a.append(ring(part_a[-1]))
        part_b.append(ring(part_b[-1]))
    late_q, part_b[1] = together(queries, part_b[1])
    mate_q = swap(late_q)
    first = call_blocks(
        functools.partial(first_kernel, ranks - 2),
        "first_blocks",
        sds((frame, width), F32),
        place,
        (*part_a[:-2], *part_b[:-2]),
        out_weight,
        range(ranks - 2),
    )
    late_v, part_a[-2] = together(mate_v, part_a[-2])
    far_v = relay(late_v)
    late_k, part_a[-1] = together(mate_k, part_a[-1])
    far_k = relay(late_k)
    late_q, part_b[-1] = together(mate_q, part_b[-1])
    far_q = relay(late_q)

    grad_a, partial = call_blocks(
        middle_kernel,
        "grad_heads_a",
        (sds((TILE, width), BF), sds((TILE, width), F32)),
        place,
        (part_a[-2], part_a[-1], part_b[-2], first),
        out_weight,
        (ranks - 2, ranks - 1),
    )
    mate_a = swap(grad_a)
    grad_b = call_blocks(
        last_kernel,
        "grad_heads_b",
        sds((TILE, width), BF),
        place,
        (part_b[-1], partial),
        out_weight,
        (ranks - 1,),
    )
    mate_b = swap(grad_b)
    wide = pltpu.VMEM((3 * frame, width), BF)
    aux, dscores = call(
        softmax_kernel,
        "softmax",
        (sds((2 * AUX, width), BF), sds((2 * (3 * TILE + text_count), width), BF)),
        2,
        (
            place, mask_lists, queries, keys, mate_k, far_k, values, mate_v, far_v,
            text_keys, text_values, grad_a, grad_b,
        ),
        (wide, wide),
    )
    mate_aux = swap(aux)
    far_a, far_b, far_aux = relay(mate_a), relay(mate_b), relay(mate_aux)
    acc = sds((frame, width), F32)
    text_acc = sds((slots, width), F32)
    accs = call(
        own_kernel,
        "own_keys",
        (acc, acc, text_acc, text_acc),
        2,
        (place, mask_lists, keys, values, sk, sv, queries, grad_a, grad_b, aux),
    )
    late_aux, far_a = together(mate_aux, far_a)
    key_acc, value_acc, keep, send = call(
        mate_kernel,
        "mate_keys",
        (acc, acc, sds((slots // 2, 2 * width), F32), sds((slots // 2, 2 * width), BF)),
        2,
        (place, mask_lists, keys, values, sk, sv, valid, mate_q, mate_a, mate_b, late_aux, *accs),
    )
    query_grads = call(
        query_kernel,
        "query_grads",
        sds((frame, width), BF),
        2,
        (place, mask_lists, keys, mate_k, far_k, text_keys, dscores),
        (wide,),
    )
    key_grads, value_grads = call(
        far_kernel,
        "far_keys",
        (sds((frame, width), BF),) * 2,
        2,
        (place, mask_lists, keys, values, far_q, far_a, far_b, far_aux, key_acc, value_acc),
    )
    stages = []
    distance = 2
    while distance < groups:
        stages.append(distance)
        distance *= 2
    for i, d in enumerate(stages):
        total = keep + swap(send, d).astype(F32)
        if i + 1 < len(stages):
            rows = total.shape[0] // 2
            keep, send = total[:rows], total[rows:].astype(BF)
    total = total.astype(BF)
    return query_grads, key_grads, value_grads, total[:, :width], total[:, width:]


def solution(mesh):
    rows = P(("seq", "rep"), "head")
    return jax.shard_map(
        local,
        mesh=mesh,
        in_specs=(rows, rows, rows, rows, P("head", None), P(None, "head"), P(None, "head"), P(), P()),
        out_specs=(rows,) * 5,
        check_vma=False,
    )
```

```python
import functools
import math

import jax
import jax.numpy as jnp
from jax import lax
from jax.experimental import pallas as pl
from jax.experimental.pallas import tpu as pltpu
from jax.sharding import PartitionSpec as P

HD = 128
TILE = 128
AUX = 16
SCALE = HD ** (-0.5)
SCALE2 = SCALE * math.log2(math.e)
OFF = 1e30
BF = jnp.bfloat16
F32 = jnp.float32
LIMIT = 16 << 20


def nt(a, b):
    return lax.dot_general(a, b, (((1,), (1,)), ((), ())), preferred_element_type=F32)


def nn(a, b):
    return lax.dot_general(a, b, (((1,), (0,)), ((), ())), preferred_element_type=F32)


def tn(a, b):
    return lax.dot_general(a, b, (((0,), (0,)), ((), ())), preferred_element_type=F32)


def lanes(h):
    return slice(h * HD, (h + 1) * HD)


def source_tile(place, lists, tile, entry):
    slab, mate = place[0], place[1]
    listed = lists[tile, entry]
    owner = lax.shift_right_logical(listed, 1)
    source = jnp.where(owner == slab, 0, jnp.where(owner == mate, 1, 2))
    return pl.multiple_of((source * 2 + (listed & 1)) * TILE, TILE)


def stack_tiles(parts, wide):
    frame = parts[0].shape[0]
    for i, part in enumerate(parts):
        wide[i * frame : (i + 1) * frame, :] = part[...]


def slot_kernel(capacity, place, owner, tk, tv, sk, sv, valid):
    count = owner.shape[1]
    slots = sk.shape[0]
    across = jnp.broadcast_to(owner[...], (count, count))
    down = across.astype(F32).T.astype(jnp.int32)
    line = lax.broadcasted_iota(jnp.int32, (count, count), 0)
    lane = lax.broadcasted_iota(jnp.int32, (count, count), 1)
    rank = jnp.sum(
        jnp.where((across == down) & (line < lane), 1, 0), axis=0, keepdims=True
    )
    slot = owner[...] * capacity + rank
    row = lax.broadcasted_iota(jnp.int32, (slots, count), 0)
    group, inside = row // capacity, row % capacity
    bits = (slots // capacity).bit_length() - 1
    offset = jnp.zeros_like(row)
    for bit in range(bits):
        offset = offset + (((group >> (bits - 1 - bit)) & 1) << (bit + 1))
    wanted = (place[0] ^ offset) * capacity + inside
    chosen = jnp.where(wanted == jnp.broadcast_to(slot, (slots, count)), 1.0, 0.0)
    live = jnp.sum(chosen, axis=1, keepdims=True)
    chosen = chosen.astype(BF)
    sk[...] = nn(chosen, tk[...]).astype(BF)
    sv[...] = nn(chosen, tv[...]).astype(BF)
    valid[...] = jnp.broadcast_to(live, valid.shape)


def gathered(wide, text, starts, cols):
    return jnp.concatenate(
        [wide[pl.ds(a, TILE), cols] for a in starts] + [text[:, cols]], axis=0
    )


def split(x, count):
    parts = []
    for _ in range(count):
        head = x.astype(BF).astype(F32)
        parts.append(head)
        x = x - head
    return parts


def block_of(place, weight, depth, step):
    ranks = weight.shape[1] // depth
    source = lax.rem(place[2] - step + ranks, ranks)
    return weight[:, pl.ds(pl.multiple_of(source * depth, 128), depth)]


def first_kernel(place, *refs):
    n = len(refs) // 2 - 1
    weight, out = refs[2 * n :]
    depth = refs[0].shape[1]
    for chunk in range(2):
        total = None
        for step in range(n):
            term = nt(refs[chunk * n + step][...], block_of(place, weight, depth, step))
            total = term if total is None else total + term
        out[chunk * TILE : (chunk + 1) * TILE, :] = total


def last_kernel(step, place, a_before, a_last, b_before, b_last, weight, first, out):
    depth = a_last.shape[1]
    before, last = (block_of(place, weight, depth, i) for i in (step - 1, step))
    for chunk, parts in enumerate(((a_before, a_last), (b_before, b_last))):
        rows = slice(chunk * TILE, (chunk + 1) * TILE)
        total = first[rows, :] + nt(parts[0][...], before)
        out[rows, :] = (total + nt(parts[1][...], last)).astype(BF)


def softmax_kernel(
    place, lists, q, k0, k1, k2, v0, v1, v2, tk, tv, g, aux, dscores, wide_k, wide_v
):
    stack_tiles((k0, k1, k2), wide_k)
    stack_tiles((v0, v1, v2), wide_v)
    row = lax.broadcasted_iota(jnp.int32, (AUX, TILE), 0)
    size = dscores.shape[0] // 2
    for tile in range(2):
        starts = [source_tile(place, lists, place[0] * 2 + tile, e) for e in range(3)]
        rows = slice(tile * TILE, (tile + 1) * TILE)
        for h in range(q.shape[1] // HD):
            cols = lanes(h)
            score = nt(gathered(wide_k, tk, starts, cols), q[rows, cols])
            top = jnp.max(score, axis=0, keepdims=True)
            weight = jnp.exp2((score - top) * SCALE2)
            total = jnp.sum(weight, axis=0, keepdims=True)
            prob = weight * (1.0 / total)
            dprob = nt(gathered(wide_v, tv, starts, cols), g[rows, cols])
            delta = jnp.sum(prob * dprob, axis=0, keepdims=True)
            dscores[tile * size : (tile + 1) * size, cols] = (prob * (dprob - delta)).astype(BF)
            lse = top * SCALE2 + jnp.log2(total)
            block = jnp.zeros((AUX, TILE), F32)
            for i, line in enumerate(split(delta, 2) + split(lse, 3)):
                block = jnp.where(row == i, jnp.broadcast_to(line, (AUX, TILE)), block)
            aux[tile * AUX : (tile + 1) * AUX, cols] = block.astype(BF)


def query_kernel(place, lists, k0, k1, k2, tk, dscores, out, wide_k):
    stack_tiles((k0, k1, k2), wide_k)
    size = dscores.shape[0] // 2
    for tile in range(2):
        starts = [source_tile(place, lists, place[0] * 2 + tile, e) for e in range(3)]
        rows = slice(tile * TILE, (tile + 1) * TILE)
        for h in range(out.shape[1] // HD):
            cols = lanes(h)
            dscore = dscores[tile * size : (tile + 1) * size, cols]
            keys = gathered(wide_k, tk, starts, cols)
            out[rows, cols] = (SCALE * tn(dscore, keys)).astype(BF)


def read_lines(aux, chunk, cols):
    lines = aux[chunk * AUX : (chunk + 1) * AUX, cols].astype(F32)
    return lines[0:1] + lines[1:2], (lines[2:3] + lines[3:4]) + lines[4:5]


def off_by(place, lists, slab, tile, key_tile):
    count = lists.shape[0]
    query_tile = slab * 2 + tile
    row = jnp.clip(query_tile, 0, count - 1)
    wanted = place[0] * 2 + key_tile
    found = (lists[row, 0] == wanted) | (lists[row, 1] == wanted) | (lists[row, 2] == wanted)
    found = found & (query_tile >= 0) & (query_tile < count)
    return jnp.where(found, 0.0, OFF)


def key_terms(offs, keys, values, q, g, aux, cols):
    lines = [read_lines(aux, i, cols) for i in range(2)]
    delta = jnp.concatenate([d for d, _ in lines], axis=1)
    lse = [l for _, l in lines]
    score = nt(keys, q) * SCALE2
    pieces = []
    for i in range(2):
        line = jnp.concatenate([lse[t] + offs[t][i] for t in range(2)], axis=1)
        pieces.append(score[i * TILE : (i + 1) * TILE] - line)
    if keys.shape[0] > 2 * TILE:
        pieces.append(score[2 * TILE :] - jnp.concatenate(lse, axis=1))
    prob = jnp.exp2(jnp.concatenate(pieces, axis=0))
    dscore = (prob * (nt(values, g) - delta)).astype(BF)
    return nn(dscore, q), nn(prob.astype(BF), g)


def all_offs(place, lists, slab):
    return [[off_by(place, lists, slab, t, i) for i in range(2)] for t in range(2)]


def own_kernel(
    place, lists, k, v, sk, sv, q, g, aux, key_acc, value_acc, text_k, text_v
):
    frame = k.shape[0]
    offs = all_offs(place, lists, place[0])
    for h in range(k.shape[1] // HD):
        cols = lanes(h)
        keys = jnp.concatenate([k[:, cols], sk[:, cols]], axis=0)
        values = jnp.concatenate([v[:, cols], sv[:, cols]], axis=0)
        dk, dv = key_terms(offs, keys, values, q[:, cols], g[:, cols], aux, cols)
        key_acc[:, cols] = dk[:frame]
        value_acc[:, cols] = dv[:frame]
        text_k[:, cols] = dk[frame:]
        text_v[:, cols] = dv[frame:]


def mate_kernel(
    place, lists, k, v, sk, sv, valid, q, g, aux, key_in, value_in, text_k, text_v,
    key_acc, value_acc, keep, send,
):
    frame, width = k.shape
    half = keep.shape[0]
    live = valid[...] > 0
    offs = all_offs(place, lists, place[1])
    for h in range(width // HD):
        cols = lanes(h)
        more = slice(width + h * HD, width + (h + 1) * HD)
        keys = jnp.concatenate([k[:, cols], sk[:, cols]], axis=0)
        values = jnp.concatenate([v[:, cols], sv[:, cols]], axis=0)
        dk, dv = key_terms(offs, keys, values, q[:, cols], g[:, cols], aux, cols)
        key_acc[:, cols] = key_in[:, cols] + dk[:frame]
        value_acc[:, cols] = value_in[:, cols] + dv[:frame]
        part_k = jnp.where(live, (text_k[:, cols] + dk[frame:]) * SCALE, 0.0)
        part_v = jnp.where(live, text_v[:, cols] + dv[frame:], 0.0)
        keep[:, cols] = part_k[:half]
        keep[:, more] = part_v[:half]
        send[:, cols] = part_k[half:].astype(BF)
        send[:, more] = part_v[half:].astype(BF)


def far_kernel(place, lists, k, v, q, g, aux, key_acc, value_acc, key_out, value_out):
    offs = all_offs(place, lists, place[3])
    for h in range(k.shape[1] // HD):
        cols = lanes(h)
        dk, dv = key_terms(offs, k[:, cols], v[:, cols], q[:, cols], g[:, cols], aux, cols)
        key_out[:, cols] = ((key_acc[:, cols] + dk) * SCALE).astype(BF)
        value_out[:, cols] = (value_acc[:, cols] + dv).astype(BF)


VMEM = pl.BlockSpec(memory_space=pltpu.VMEM)
SMEM = pl.BlockSpec(memory_space=pltpu.SMEM)


def call(kernel, name, outs, scalars, arrays, scratch=()):
    return pl.pallas_call(
        kernel,
        name=name,
        out_shape=outs,
        in_specs=[SMEM] * scalars + [VMEM] * (len(arrays) - scalars),
        out_specs=jax.tree.map(lambda _: VMEM, outs),
        scratch_shapes=list(scratch),
        compiler_params=pltpu.CompilerParams(vmem_limit_bytes=LIMIT),
    )(*arrays)


def together(*arrays):
    return lax.optimization_barrier(arrays)


def local(
    queries, keys, values, grad_output, out_weight, text_keys, text_values, mask_lists, text_owner
):
    frame, width = queries.shape
    text_count = text_keys.shape[0]
    both = ("seq", "rep")
    seqs, reps, ranks = lax.axis_size("seq"), lax.axis_size("rep"), lax.axis_size("head")
    groups = seqs * reps
    slab = lax.axis_index(both)
    mate = slab ^ 1
    other = jnp.where(slab & 1, slab + 1, slab - 1)
    place = jnp.stack([slab, mate, lax.axis_index("head"), other]).astype(jnp.int32)

    def swap(x, distance=1):
        return lax.ppermute(x, both, [(i, i ^ distance) for i in range(groups)])

    def relay(x):
        turns = [(i, (i + 2 - 4 * (i % 2)) % groups) for i in range(groups)]
        return lax.ppermute(x, both, turns)

    def ring(x, way=1):
        return lax.ppermute(x, "head", [(i, (i + way) % ranks) for i in range(ranks)])

    capacity = 2 * text_count // groups
    slots = groups // 2 * capacity
    sds = jax.ShapeDtypeStruct
    sk, sv, valid = call(
        functools.partial(slot_kernel, capacity),
        "slots",
        (sds((slots, width), BF),) * 2 + (sds((slots, HD), F32),),
        1,
        (place, text_owner.reshape(1, text_count), text_keys, text_values),
    )
    part_a, part_b = [grad_output[:TILE]], [grad_output[TILE:]]
    mate_v, mate_k, mate_q = swap(values), swap(keys), swap(queries)
    part_a.append(ring(part_a[0]))
    part_b.append(ring(part_b[0]))
    for step in range(ranks - 2):
        if step == ranks - 3:
            first = call(
                first_kernel,
                "first_blocks",
                sds((frame, width), F32),
                1,
                (place, *part_a[:-1], *part_b[:-1], out_weight),
            )
            part_a[-1], mate_v = together(part_a[-1], mate_v)
            part_b[-1], mate_k, first = together(part_b[-1], mate_k, first)
        part_a.append(ring(part_a[-1]))
        part_b.append(ring(part_b[-1]))
    part_a[-1], mate_v, mate_k = together(part_a[-1], mate_v, mate_k)
    far_v, far_k = relay(mate_v), relay(mate_k)

    grad = call(
        functools.partial(last_kernel, ranks - 1),
        "grad_heads",
        sds((frame, width), BF),
        1,
        (place, *part_a[-2:], *part_b[-2:], out_weight, first),
    )
    late_grad, mate_q = together(grad, mate_q)
    mate_g = swap(late_grad)
    far_q = relay(mate_q)
    wide = pltpu.VMEM((3 * frame, width), BF)
    aux, dscores = call(
        softmax_kernel,
        "softmax",
        (sds((2 * AUX, width), BF), sds((2 * (3 * TILE + text_count), width), BF)),
        2,
        (
            place, mask_lists, queries, keys, mate_k, far_k, values, mate_v, far_v,
            text_keys, text_values, grad,
        ),
        (wide, wide),
    )
    mate_aux = swap(aux)
    far_g, far_aux = relay(mate_g), relay(mate_aux)
    own_aux, far_q = together(aux, far_q)
    acc = sds((frame, width), F32)
    text_acc = sds((slots, width), F32)
    accs = call(
        own_kernel,
        "own_keys",
        (acc, acc, text_acc, text_acc),
        2,
        (place, mask_lists, keys, values, sk, sv, queries, grad, own_aux),
    )
    key_acc, value_acc, keep, send = call(
        mate_kernel,
        "mate_keys",
        (acc, acc, sds((slots // 2, 2 * width), F32), sds((slots // 2, 2 * width), BF)),
        2,
        (place, mask_lists, keys, values, sk, sv, valid, mate_q, mate_g, mate_aux, *accs),
    )
    query_grads = call(
        query_kernel,
        "query_grads",
        sds((frame, width), BF),
        2,
        (place, mask_lists, keys, mate_k, far_k, text_keys, dscores),
        (wide,),
    )
    key_grads, value_grads = call(
        far_kernel,
        "far_keys",
        (sds((frame, width), BF),) * 2,
        2,
        (place, mask_lists, keys, values, far_q, far_g, far_aux, key_acc, value_acc),
    )
    stages = []
    distance = 2
    while distance < groups:
        stages.append(distance)
        distance *= 2
    for i, d in enumerate(stages):
        total = keep + swap(send, d).astype(F32)
        if i + 1 < len(stages):
            rows = total.shape[0] // 2
            keep, send = total[:rows], total[rows:].astype(BF)
    total = total.astype(BF)
    return query_grads, key_grads, value_grads, total[:, :width], total[:, width:]


def solution(mesh):
    rows = P(("seq", "rep"), "head")
    return jax.shard_map(
        local,
        mesh=mesh,
        in_specs=(rows, rows, rows, rows, P("head", None), P(None, "head"), P(None, "head"), P(), P()),
        out_specs=(rows,) * 5,
        check_vma=False,
    )
```

```python
import functools
import math

import jax
import jax.numpy as jnp
from jax import lax
from jax.experimental import pallas as pl
from jax.experimental.pallas import tpu as pltpu
from jax.sharding import PartitionSpec as P

HD = 128
TILE = 128
AUX = 16
SCALE = HD ** (-0.5)
SCALE2 = SCALE * math.log2(math.e)
OFF = 1e30
GROUP = 3
PAIRS = 3
BF = jnp.bfloat16
F32 = jnp.float32
LIMIT = 16 << 20


def nt(a, b):
    return lax.dot_general(a, b, (((1,), (1,)), ((), ())), preferred_element_type=F32)


def nn(a, b):
    return lax.dot_general(a, b, (((1,), (0,)), ((), ())), preferred_element_type=F32)


def tn(a, b):
    return lax.dot_general(a, b, (((0,), (0,)), ((), ())), preferred_element_type=F32)


def lanes(h):
    return slice(h * HD, (h + 1) * HD)


def source_tile(place, lists, tile, entry):
    slab, mate = place[0], place[1]
    listed = lists[entry, tile]
    owner = lax.shift_right_logical(listed, 1)
    source = jnp.where(owner == slab, 0, jnp.where(owner == mate, 1, 2))
    return pl.multiple_of((source * 2 + (listed & 1)) * TILE, TILE)


def stack_tiles(parts, wide):
    frame = parts[0].shape[0]
    for i, part in enumerate(parts):
        wide[i * frame : (i + 1) * frame, :] = part[...]


def slot_kernel(capacity, place, owner, tk, tv, sk, sv, valid):
    count = owner.shape[1]
    slots = sk.shape[0]
    across = jnp.broadcast_to(owner[...], (count, count))
    down = across.astype(F32).T.astype(jnp.int32)
    line = lax.broadcasted_iota(jnp.int32, (count, count), 0)
    lane = lax.broadcasted_iota(jnp.int32, (count, count), 1)
    rank = jnp.sum(
        jnp.where((across == down) & (line < lane), 1, 0), axis=0, keepdims=True
    )
    slot = owner[...] * capacity + rank
    row = lax.broadcasted_iota(jnp.int32, (slots, count), 0)
    group, inside = row // capacity, row % capacity
    bits = (slots // capacity).bit_length() - 1
    offset = jnp.zeros_like(row)
    for bit in range(bits):
        offset = offset + (((group >> (bits - 1 - bit)) & 1) << (bit + 1))
    wanted = (place[0] ^ offset) * capacity + inside
    chosen = jnp.where(wanted == jnp.broadcast_to(slot, (slots, count)), 1.0, 0.0)
    live = jnp.sum(chosen, axis=1, keepdims=True)
    chosen = chosen.astype(BF)
    sk[...] = nn(chosen, tk[...]).astype(BF)
    sv[...] = nn(chosen, tv[...]).astype(BF)
    valid[...] = jnp.broadcast_to(live, valid.shape)


def gathered(wide, text, starts, cols):
    return jnp.concatenate(
        [wide[pl.ds(a, TILE), cols] for a in starts] + [text[:, cols]], axis=0
    )


def split(x, count):
    parts = []
    for _ in range(count):
        head = x.astype(BF).astype(F32)
        parts.append(head)
        x = x - head
    return parts


def block_of(place, weight, depth, step):
    ranks = weight.shape[1] // depth
    source = lax.rem(place[2] - step + ranks, ranks)
    return weight[:, pl.ds(pl.multiple_of(source * depth, 128), depth)]


def first_kernel(place, *refs):
    n = len(refs) // 2 - 1
    weight, out = refs[2 * n :]
    depth = refs[0].shape[1]
    for chunk in range(2):
        total = None
        for step in range(n):
            term = nt(refs[chunk * n + step][...], block_of(place, weight, depth, step))
            total = term if total is None else total + term
        out[chunk * TILE : (chunk + 1) * TILE, :] = total


def second_kernel(step, place, a_before, b_before, weight, first, out):
    block = block_of(place, weight, a_before.shape[1], step)
    for chunk, part in enumerate((a_before, b_before)):
        rows = slice(chunk * TILE, (chunk + 1) * TILE)
        out[rows, :] = first[rows, :] + nt(part[...], block)


def last_kernel(step, place, a_last, b_last, weight, second, out):
    block = block_of(place, weight, a_last.shape[1], step)
    for chunk, part in enumerate((a_last, b_last)):
        rows = slice(chunk * TILE, (chunk + 1) * TILE)
        out[rows, :] = (second[rows, :] + nt(part[...], block)).astype(BF)


def softmax_kernel(
    place, lists, q, k0, k1, k2, v0, v1, v2, tk, tv, g, aux, dscores, wide_k, wide_v
):
    stack_tiles((k0, k1, k2), wide_k)
    stack_tiles((v0, v1, v2), wide_v)
    row = lax.broadcasted_iota(jnp.int32, (AUX, TILE), 0)
    size = dscores.shape[0] // 2
    jobs = []
    for tile in range(2):
        starts = [source_tile(place, lists, place[0] * 2 + tile, e) for e in range(3)]
        rows = slice(tile * TILE, (tile + 1) * TILE)
        jobs += [(tile, rows, starts, lanes(h)) for h in range(q.shape[1] // HD)]
    for first in range(0, len(jobs), PAIRS):
        group = jobs[first : first + PAIRS]
        scores = [nt(gathered(wide_k, tk, at, cols), q[rows, cols]) for _, rows, at, cols in group]
        dprobs = [nt(gathered(wide_v, tv, at, cols), g[rows, cols]) for _, rows, at, cols in group]
        for (tile, _, _, cols), score, dprob in zip(group, scores, dprobs):
            top = jnp.max(score, axis=0, keepdims=True)
            weight = jnp.exp2((score - top) * SCALE2)
            total = jnp.sum(weight, axis=0, keepdims=True)
            prob = weight * (1.0 / total)
            delta = jnp.sum(prob * dprob, axis=0, keepdims=True)
            dscores[tile * size : (tile + 1) * size, cols] = (prob * (dprob - delta)).astype(BF)
            lse = top * SCALE2 + jnp.log2(total)
            block = jnp.zeros((AUX, TILE), F32)
            for i, line in enumerate(split(delta, 2) + split(lse, 3)):
                block = jnp.where(row == i, jnp.broadcast_to(line, (AUX, TILE)), block)
            aux[tile * AUX : (tile + 1) * AUX, cols] = block.astype(BF)


def query_kernel(place, lists, k0, k1, k2, tk, dscores, out, wide_k):
    stack_tiles((k0, k1, k2), wide_k)
    size = dscores.shape[0] // 2
    for tile in range(2):
        starts = [source_tile(place, lists, place[0] * 2 + tile, e) for e in range(3)]
        rows = slice(tile * TILE, (tile + 1) * TILE)
        for h in range(out.shape[1] // HD):
            cols = lanes(h)
            dscore = dscores[tile * size : (tile + 1) * size, cols]
            keys = gathered(wide_k, tk, starts, cols)
            out[rows, cols] = (SCALE * tn(dscore, keys)).astype(BF)


def read_lines(aux, chunk, cols):
    lines = aux[chunk * AUX : (chunk + 1) * AUX, cols].astype(F32)
    return lines[0:1] + lines[1:2], (lines[2:3] + lines[3:4]) + lines[4:5]


def off_by(place, lists, slab, tile, key_tile):
    count = lists.shape[1]
    query_tile = slab * 2 + tile
    row = jnp.clip(query_tile, 0, count - 1)
    wanted = place[0] * 2 + key_tile
    found = (lists[0, row] == wanted) | (lists[1, row] == wanted) | (lists[2, row] == wanted)
    found = found & (query_tile >= 0) & (query_tile < count)
    return jnp.where(found, 0.0, OFF)


def key_terms(offs, keys, values, q, g, aux, emit):
    heads = [lanes(h) for h in range(q.shape[1] // HD)]
    for first in range(0, len(heads), GROUP):
        group = heads[first : first + GROUP]
        q_rows = [q[:, cols] for cols in group]
        g_rows = [g[:, cols] for cols in group]
        scores = [nt(keys(cols), rows) for cols, rows in zip(group, q_rows)]
        dprobs = [nt(values(cols), rows) for cols, rows in zip(group, g_rows)]
        probs, dscores = [], []
        for cols, score, dprob in zip(group, scores, dprobs):
            lines = [read_lines(aux, i, cols) for i in range(2)]
            delta = jnp.concatenate([d for d, _ in lines], axis=1)
            lse = [l for _, l in lines]
            score = score * SCALE2
            pieces = []
            if offs is not None:
                for i in range(2):
                    line = jnp.concatenate([lse[t] + offs[t][i] for t in range(2)], axis=1)
                    pieces.append(score[i * TILE : (i + 1) * TILE] - line)
            done = len(pieces) * TILE
            if score.shape[0] > done:
                pieces.append(score[done:] - jnp.concatenate(lse, axis=1))
            prob = jnp.exp2(jnp.concatenate(pieces, axis=0))
            probs.append(prob.astype(BF))
            dscores.append((prob * (dprob - delta)).astype(BF))
        sums_k = [nn(dscore, rows) for dscore, rows in zip(dscores, q_rows)]
        sums_v = [nn(prob, rows) for prob, rows in zip(probs, g_rows)]
        for cols, dk, dv in zip(group, sums_k, sums_v):
            emit(cols, dk, dv)


def all_offs(place, lists, slab):
    return [[off_by(place, lists, slab, t, i) for i in range(2)] for t in range(2)]


def pair(top, low):
    return lambda cols: jnp.concatenate([top[:, cols], low[:, cols]], axis=0)


def own_kernel(
    place, lists, k, v, sk, sv, q, g, aux, key_acc, value_acc, text_k, text_v
):
    frame = k.shape[0]

    def emit(cols, dk, dv):
        key_acc[:, cols] = dk[:frame]
        value_acc[:, cols] = dv[:frame]
        text_k[:, cols] = dk[frame:]
        text_v[:, cols] = dv[frame:]

    offs = all_offs(place, lists, place[0])
    key_terms(offs, pair(k, sk), pair(v, sv), q, g, aux, emit)


def whole(ref):
    return lambda cols: ref[:, cols]


def text_kernel(sk, sv, valid, q, g, aux, text_k, text_v, keep, send, message):
    width = q.shape[1]
    half = keep.shape[0]
    live = valid[...] > 0
    message[: g.shape[0], :] = g[...]
    message[g.shape[0] :, :] = aux[...]

    def emit(cols, dk, dv):
        more = slice(cols.start + width, cols.stop + width)
        part_k = jnp.where(live, (text_k[:, cols] + dk) * SCALE, 0.0)
        part_v = jnp.where(live, text_v[:, cols] + dv, 0.0)
        keep[:, cols] = part_k[:half]
        keep[:, more] = part_v[:half]
        send[:, cols] = part_k[half:].astype(BF)
        send[:, more] = part_v[half:].astype(BF)

    key_terms(None, whole(sk), whole(sv), q, g, aux, emit)


def mate_kernel(place, lists, k, v, q, g, aux, key_in, value_in, key_acc, value_acc):
    def emit(cols, dk, dv):
        key_acc[:, cols] = key_in[:, cols] + dk
        value_acc[:, cols] = value_in[:, cols] + dv

    key_terms(all_offs(place, lists, place[1]), whole(k), whole(v), q, g, aux, emit)


def far_kernel(place, lists, k, v, q, message, key_acc, value_acc, key_out, value_out):
    rows = q.shape[0]
    g, aux = message.at[:rows], message.at[rows:]

    def emit(cols, dk, dv):
        key_out[:, cols] = ((key_acc[:, cols] + dk) * SCALE).astype(BF)
        value_out[:, cols] = (value_acc[:, cols] + dv).astype(BF)

    key_terms(all_offs(place, lists, place[3]), whole(k), whole(v), q, g, aux, emit)


def add_kernel(keep, arrived, more, send):
    rows = more.shape[0]
    more[...] = keep[:rows, :] + arrived[:rows, :].astype(F32)
    send[...] = (keep[rows:, :] + arrived[rows:, :].astype(F32)).astype(BF)


def finish_kernel(keep, arrived, key_out, value_out):
    width = key_out.shape[1]
    total = (keep[...] + arrived[...].astype(F32)).astype(BF)
    key_out[...] = total[:, :width]
    value_out[...] = total[:, width:]


VMEM = pl.BlockSpec(memory_space=pltpu.VMEM)
SMEM = pl.BlockSpec(memory_space=pltpu.SMEM)


def call(kernel, name, outs, scalars, arrays, scratch=()):
    return pl.pallas_call(
        kernel,
        name=name,
        out_shape=outs,
        in_specs=[SMEM] * scalars + [VMEM] * (len(arrays) - scalars),
        out_specs=jax.tree.map(lambda _: VMEM, outs),
        scratch_shapes=list(scratch),
        compiler_params=pltpu.CompilerParams(vmem_limit_bytes=LIMIT),
    )(*arrays)


def together(*arrays):
    return lax.optimization_barrier(arrays)


def local(
    queries, keys, values, grad_output, out_weight, text_keys, text_values, mask_lists, text_owner
):
    frame, width = queries.shape
    text_count = text_keys.shape[0]
    both = ("seq", "rep")
    seqs, reps, ranks = lax.axis_size("seq"), lax.axis_size("rep"), lax.axis_size("head")
    groups = seqs * reps
    lists = mask_lists.T
    slab = lax.axis_index(both)
    mate = slab ^ 1
    other = jnp.where(slab & 1, slab + 1, slab - 1)
    place = jnp.stack([slab, mate, lax.axis_index("head"), other]).astype(jnp.int32)

    def swap(x, distance=1):
        return lax.ppermute(x, both, [(i, i ^ distance) for i in range(groups)])

    def relay(x):
        turns = [(i, (i + 2 - 4 * (i % 2)) % groups) for i in range(groups)]
        return lax.ppermute(x, both, turns)

    def ring(x, way=1):
        return lax.ppermute(x, "head", [(i, (i + way) % ranks) for i in range(ranks)])

    capacity = 2 * text_count // groups
    slots = groups // 2 * capacity
    sds = jax.ShapeDtypeStruct
    sk, sv, valid = call(
        functools.partial(slot_kernel, capacity),
        "slots",
        (sds((slots, width), BF),) * 2 + (sds((slots, HD), F32),),
        1,
        (place, text_owner.reshape(1, text_count), text_keys, text_values),
    )
    start_a, late_grad = together(grad_output[:TILE], grad_output)
    part_a, part_b = [start_a], [late_grad[TILE:]]
    mate_v, mate_k, mate_q = swap(values), swap(keys), swap(queries)
    part_a.append(ring(part_a[0]))
    part_b.append(ring(part_b[0]))
    for step in range(ranks - 2):
        if step == ranks - 3:
            first = call(
                first_kernel,
                "first_blocks",
                sds((frame, width), F32),
                1,
                (place, *part_a[:-1], *part_b[:-1], out_weight),
            )
            part_a[-1], mate_v = together(part_a[-1], mate_v)
            part_b[-1], mate_k, first = together(part_b[-1], mate_k, first)
        part_a.append(ring(part_a[-1]))
        part_b.append(ring(part_b[-1]))
    part_a[-1], mate_v, mate_k = together(part_a[-1], mate_v, mate_k)
    far_v, far_k = relay(mate_v), relay(mate_k)

    second = call(
        functools.partial(second_kernel, ranks - 2),
        "second_blocks",
        sds((frame, width), F32),
        1,
        (place, part_a[-2], part_b[-2], out_weight, first),
    )
    grad = call(
        functools.partial(last_kernel, ranks - 1),
        "grad_heads",
        sds((frame, width), BF),
        1,
        (place, part_a[-1], part_b[-1], out_weight, second),
    )
    late_grad, mate_q = together(grad, mate_q)
    mate_g = swap(late_grad)
    far_q = relay(mate_q)
    far_k, sk = together(far_k, sk)
    wide = pltpu.VMEM((3 * frame, width), BF)
    aux, dscores = call(
        softmax_kernel,
        "softmax",
        (sds((2 * AUX, width), BF), sds((2 * (3 * TILE + text_count), width), BF)),
        2,
        (
            place, lists, queries, keys, mate_k, far_k, values, mate_v, far_v,
            text_keys, text_values, grad,
        ),
        (wide, wide),
    )
    mate_aux = swap(aux)
    own_aux, far_q = together(aux, far_q)
    acc = sds((frame, width), F32)
    text_acc = sds((slots, width), F32)
    accs = call(
        own_kernel,
        "own_keys",
        (acc, acc, text_acc, text_acc),
        2,
        (place, lists, keys, values, sk, sv, queries, grad, own_aux),
    )
    key_acc, value_acc, text_k, text_v = accs
    keep, send, message = call(
        text_kernel,
        "text_slots",
        (
            sds((slots // 2, 2 * width), F32),
            sds((slots // 2, 2 * width), BF),
            sds((frame + 2 * AUX, width), BF),
        ),
        0,
        (sk, sv, valid, mate_q, mate_g, mate_aux, text_k, text_v),
    )
    far_message = relay(message)
    key_acc, value_acc = call(
        mate_kernel,
        "mate_keys",
        (acc, acc),
        2,
        (place, lists, keys, values, mate_q, mate_g, mate_aux, key_acc, value_acc),
    )
    query_grads = call(
        query_kernel,
        "query_grads",
        sds((frame, width), BF),
        2,
        (place, lists, keys, mate_k, far_k, text_keys, dscores),
        (wide,),
    )
    key_grads, value_grads = call(
        far_kernel,
        "far_keys",
        (sds((frame, width), BF),) * 2,
        2,
        (place, lists, keys, values, far_q, far_message, key_acc, value_acc),
    )
    stages = []
    distance = 2
    while distance < groups:
        stages.append(distance)
        distance *= 2
    for i, d in enumerate(stages):
        arrived = swap(send, d)
        rows = keep.shape[0] // 2
        if i + 1 < len(stages):
            keep, send = call(
                add_kernel,
                f"add_slots_{i}",
                (sds((rows, 2 * width), F32), sds((rows, 2 * width), BF)),
                0,
                (keep, arrived),
            )
    text_key_grads, text_value_grads = call(
        finish_kernel, "finish_slots", (sds((2 * rows, width), BF),) * 2, 0, (keep, arrived)
    )
    return query_grads, key_grads, value_grads, text_key_grads, text_value_grads


def solution(mesh):
    rows = P(("seq", "rep"), "head")
    return jax.shard_map(
        local,
        mesh=mesh,
        in_specs=(rows, rows, rows, rows, P("head", None), P(None, "head"), P(None, "head"), P(), P()),
        out_specs=(rows,) * 5,
        check_vma=False,
    )
```

```python
import functools
import math

import jax
import jax.numpy as jnp
from jax import lax
from jax.experimental import pallas as pl
from jax.experimental.pallas import tpu as pltpu
from jax.sharding import PartitionSpec as P

HD = 128
TILE = 128
AUX = 16
SCALE = HD ** (-0.5)
SCALE2 = SCALE * math.log2(math.e)
OFF = 1e30
GROUP = 3
PAIRS = 3
BF = jnp.bfloat16
F32 = jnp.float32
LIMIT = 16 << 20


def nt(a, b):
    return lax.dot_general(a, b, (((1,), (1,)), ((), ())), preferred_element_type=F32)


def nn(a, b):
    return lax.dot_general(a, b, (((1,), (0,)), ((), ())), preferred_element_type=F32)


def tn(a, b):
    return lax.dot_general(a, b, (((0,), (0,)), ((), ())), preferred_element_type=F32)


def lanes(h):
    return slice(h * HD, (h + 1) * HD)


def source_tile(place, lists, tile, entry):
    slab, mate = place[0], place[1]
    listed = lists[entry, tile]
    owner = lax.shift_right_logical(listed, 1)
    source = jnp.where(owner == slab, 0, jnp.where(owner == mate, 1, 2))
    return pl.multiple_of((source * 2 + (listed & 1)) * TILE, TILE)


def stack_tiles(parts, wide):
    frame = parts[0].shape[0]
    for i, part in enumerate(parts):
        wide[i * frame : (i + 1) * frame, :] = part[...]


def slot_kernel(capacity, place, owner, tk, tv, sk, sv, valid):
    count = owner.shape[1]
    slots = sk.shape[0]
    across = jnp.broadcast_to(owner[...], (count, count))
    down = across.astype(F32).T.astype(jnp.int32)
    line = lax.broadcasted_iota(jnp.int32, (count, count), 0)
    lane = lax.broadcasted_iota(jnp.int32, (count, count), 1)
    rank = jnp.sum(
        jnp.where((across == down) & (line < lane), 1, 0), axis=0, keepdims=True
    )
    slot = owner[...] * capacity + rank
    row = lax.broadcasted_iota(jnp.int32, (slots, count), 0)
    group, inside = row // capacity, row % capacity
    bits = (slots // capacity).bit_length() - 1
    offset = jnp.zeros_like(row)
    for bit in range(bits):
        offset = offset + (((group >> (bits - 1 - bit)) & 1) << (bit + 1))
    wanted = (place[0] ^ offset) * capacity + inside
    chosen = jnp.where(wanted == jnp.broadcast_to(slot, (slots, count)), 1.0, 0.0)
    live = jnp.sum(chosen, axis=1, keepdims=True)
    chosen = chosen.astype(BF)
    sk[...] = nn(chosen, tk[...]).astype(BF)
    sv[...] = nn(chosen, tv[...]).astype(BF)
    valid[...] = jnp.broadcast_to(live, valid.shape)


def gathered(wide, text, starts, cols):
    return jnp.concatenate(
        [wide[pl.ds(a, TILE), cols] for a in starts] + [text[:, cols]], axis=0
    )


def split(x, count):
    parts = []
    for _ in range(count):
        head = x.astype(BF).astype(F32)
        parts.append(head)
        x = x - head
    return parts


def block_of(place, weight, depth, step):
    ranks = weight.shape[1] // depth
    source = place[4 + lax.rem(place[2] - step + ranks, ranks)]
    return weight[:, pl.ds(pl.multiple_of(source * depth, 128), depth)]


def first_kernel(place, *refs):
    n = len(refs) // 2 - 1
    weight, out = refs[2 * n :]
    depth = refs[0].shape[1]
    for chunk in range(2):
        total = None
        for step in range(n):
            term = nt(refs[chunk * n + step][...], block_of(place, weight, depth, step))
            total = term if total is None else total + term
        out[chunk * TILE : (chunk + 1) * TILE, :] = total


def second_kernel(step, place, a_before, b_before, weight, first, out):
    block = block_of(place, weight, a_before.shape[1], step)
    for chunk, part in enumerate((a_before, b_before)):
        rows = slice(chunk * TILE, (chunk + 1) * TILE)
        out[rows, :] = first[rows, :] + nt(part[...], block)


def last_kernel(step, chunk, place, last, weight, second, out):
    block = block_of(place, weight, last.shape[1], step)
    rows = slice(chunk * TILE, (chunk + 1) * TILE)
    out[...] = (second[rows, :] + nt(last[...], block)).astype(BF)


def softmax_kernel(
    place, lists, q, k0, k1, k2, v0, v1, v2, tk, tv, ga, gb, aux, dscores, wide_k, wide_v
):
    stack_tiles((k0, k1, k2), wide_k)
    stack_tiles((v0, v1, v2), wide_v)
    row = lax.broadcasted_iota(jnp.int32, (AUX, TILE), 0)
    size = dscores.shape[0] // 2
    jobs = []
    for tile in range(2):
        starts = [source_tile(place, lists, place[0] * 2 + tile, e) for e in range(3)]
        rows = slice(tile * TILE, (tile + 1) * TILE)
        jobs += [(tile, rows, starts, lanes(h)) for h in range(q.shape[1] // HD)]
    for first in range(0, len(jobs), PAIRS):
        group = jobs[first : first + PAIRS]
        scores = [nt(gathered(wide_k, tk, at, cols), q[rows, cols]) for _, rows, at, cols in group]
        dprobs = [nt(gathered(wide_v, tv, at, cols), (ga, gb)[tile][:, cols]) for tile, _, at, cols in group]
        for (tile, _, _, cols), score, dprob in zip(group, scores, dprobs):
            top = jnp.max(score, axis=0, keepdims=True)
            weight = jnp.exp2((score - top) * SCALE2)
            total = jnp.sum(weight, axis=0, keepdims=True)
            prob = weight * (1.0 / total)
            delta = jnp.sum(prob * dprob, axis=0, keepdims=True)
            dscores[tile * size : (tile + 1) * size, cols] = (prob * (dprob - delta)).astype(BF)
            lse = top * SCALE2 + jnp.log2(total)
            block = jnp.zeros((AUX, TILE), F32)
            for i, line in enumerate(split(delta, 2) + split(lse, 3)):
                block = jnp.where(row == i, jnp.broadcast_to(line, (AUX, TILE)), block)
            aux[tile * AUX : (tile + 1) * AUX, cols] = block.astype(BF)


def query_kernel(place, lists, k0, k1, k2, tk, dscores, out, wide_k):
    stack_tiles((k0, k1, k2), wide_k)
    size = dscores.shape[0] // 2
    for tile in range(2):
        starts = [source_tile(place, lists, place[0] * 2 + tile, e) for e in range(3)]
        rows = slice(tile * TILE, (tile + 1) * TILE)
        for h in range(out.shape[1] // HD):
            cols = lanes(h)
            dscore = dscores[tile * size : (tile + 1) * size, cols]
            keys = gathered(wide_k, tk, starts, cols)
            out[rows, cols] = (SCALE * tn(dscore, keys)).astype(BF)


def read_lines(aux, chunk, cols):
    lines = aux[chunk * AUX : (chunk + 1) * AUX, cols].astype(F32)
    return lines[0:1] + lines[1:2], (lines[2:3] + lines[3:4]) + lines[4:5]


def off_by(place, lists, slab, tile, key_tile):
    count = lists.shape[1]
    query_tile = slab * 2 + tile
    row = jnp.clip(query_tile, 0, count - 1)
    wanted = place[0] * 2 + key_tile
    found = (lists[0, row] == wanted) | (lists[1, row] == wanted) | (lists[2, row] == wanted)
    found = found & (query_tile >= 0) & (query_tile < count)
    return jnp.where(found, 0.0, OFF)


def key_terms(offs, keys, values, q, ga, gb, aux, emit):
    heads = [lanes(h) for h in range(q.shape[1] // HD)]
    for first in range(0, len(heads), GROUP):
        group = heads[first : first + GROUP]
        q_rows = [q[:, cols] for cols in group]
        g_rows = [jnp.concatenate([ga[:, cols], gb[:, cols]], axis=0) for cols in group]
        scores = [nt(keys(cols), rows) for cols, rows in zip(group, q_rows)]
        dprobs = [nt(values(cols), rows) for cols, rows in zip(group, g_rows)]
        probs, dscores = [], []
        for cols, score, dprob in zip(group, scores, dprobs):
            lines = [read_lines(aux, i, cols) for i in range(2)]
            delta = jnp.concatenate([d for d, _ in lines], axis=1)
            lse = [l for _, l in lines]
            score = score * SCALE2
            pieces = []
            if offs is not None:
                for i in range(2):
                    line = jnp.concatenate([lse[t] + offs[t][i] for t in range(2)], axis=1)
                    pieces.append(score[i * TILE : (i + 1) * TILE] - line)
            done = len(pieces) * TILE
            if score.shape[0] > done:
                pieces.append(score[done:] - jnp.concatenate(lse, axis=1))
            prob = jnp.exp2(jnp.concatenate(pieces, axis=0))
            probs.append(prob.astype(BF))
            dscores.append((prob * (dprob - delta)).astype(BF))
        sums_k = [nn(dscore, rows) for dscore, rows in zip(dscores, q_rows)]
        sums_v = [nn(prob, rows) for prob, rows in zip(probs, g_rows)]
        for cols, dk, dv in zip(group, sums_k, sums_v):
            emit(cols, dk, dv)


def all_offs(place, lists, slab):
    return [[off_by(place, lists, slab, t, i) for i in range(2)] for t in range(2)]


def pair(top, low):
    return lambda cols: jnp.concatenate([top[:, cols], low[:, cols]], axis=0)


def own_kernel(
    place, lists, k, v, sk, sv, q, ga, gb, aux, key_acc, value_acc, text_k, text_v
):
    frame = k.shape[0]

    def emit(cols, dk, dv):
        key_acc[:, cols] = dk[:frame]
        value_acc[:, cols] = dv[:frame]
        text_k[:, cols] = dk[frame:]
        text_v[:, cols] = dv[frame:]

    offs = all_offs(place, lists, place[0])
    key_terms(offs, pair(k, sk), pair(v, sv), q, ga, gb, aux, emit)


def whole(ref):
    return lambda cols: ref[:, cols]


def text_kernel(sk, sv, valid, q, ga, gb, aux, text_k, text_v, keep, send, message):
    width = q.shape[1]
    half = keep.shape[0]
    live = valid[...] > 0
    message[:TILE, :] = gb[...]
    message[TILE:, :] = aux[...]

    def emit(cols, dk, dv):
        more = slice(cols.start + width, cols.stop + width)
        part_k = jnp.where(live, (text_k[:, cols] + dk) * SCALE, 0.0)
        part_v = jnp.where(live, text_v[:, cols] + dv, 0.0)
        keep[:, cols] = part_k[:half]
        keep[:, more] = part_v[:half]
        send[:, cols] = part_k[half:].astype(BF)
        send[:, more] = part_v[half:].astype(BF)

    key_terms(None, whole(sk), whole(sv), q, ga, gb, aux, emit)


def mate_kernel(place, lists, k, v, q, ga, gb, aux, key_in, value_in, key_acc, value_acc):
    def emit(cols, dk, dv):
        key_acc[:, cols] = key_in[:, cols] + dk
        value_acc[:, cols] = value_in[:, cols] + dv

    key_terms(all_offs(place, lists, place[1]), whole(k), whole(v), q, ga, gb, aux, emit)


def far_kernel(place, lists, k, v, q, ga, message, key_acc, value_acc, key_out, value_out):
    gb, aux = message.at[:TILE], message.at[TILE:]

    def emit(cols, dk, dv):
        key_out[:, cols] = ((key_acc[:, cols] + dk) * SCALE).astype(BF)
        value_out[:, cols] = (value_acc[:, cols] + dv).astype(BF)

    key_terms(all_offs(place, lists, place[3]), whole(k), whole(v), q, ga, gb, aux, emit)


def add_kernel(keep, arrived, more, send):
    rows = more.shape[0]
    more[...] = keep[:rows, :] + arrived[:rows, :].astype(F32)
    send[...] = (keep[rows:, :] + arrived[rows:, :].astype(F32)).astype(BF)


def finish_kernel(keep, arrived, key_out, value_out):
    width = key_out.shape[1]
    total = (keep[...] + arrived[...].astype(F32)).astype(BF)
    key_out[...] = total[:, :width]
    value_out[...] = total[:, width:]


VMEM = pl.BlockSpec(memory_space=pltpu.VMEM)
SMEM = pl.BlockSpec(memory_space=pltpu.SMEM)


def call(kernel, name, outs, scalars, arrays, scratch=()):
    return pl.pallas_call(
        kernel,
        name=name,
        out_shape=outs,
        in_specs=[SMEM] * scalars + [VMEM] * (len(arrays) - scalars),
        out_specs=jax.tree.map(lambda _: VMEM, outs),
        scratch_shapes=list(scratch),
        compiler_params=pltpu.CompilerParams(vmem_limit_bytes=LIMIT),
    )(*arrays)


def together(*arrays):
    return lax.optimization_barrier(arrays)


def local(
    queries, keys, values, grad_output, out_weight, text_keys, text_values, mask_lists, text_owner
):
    frame, width = queries.shape
    text_count = text_keys.shape[0]
    both = ("seq", "rep")
    seqs, reps, ranks = lax.axis_size("seq"), lax.axis_size("rep"), lax.axis_size("head")
    groups = seqs * reps
    lists = mask_lists.T
    slab = lax.axis_index(both)
    mate = slab ^ 1
    other = jnp.where(slab & 1, slab + 1, slab - 1)
    order = list(range(0, ranks, 2)) + list(range(1, ranks, 2))[::-1]
    seat = sum(
        jnp.where(lax.axis_index("head") == rank, i, 0) for i, rank in enumerate(order)
    )
    place = jnp.stack([slab, mate, seat, other, *order]).astype(jnp.int32)

    def swap(x, distance=1):
        return lax.ppermute(x, both, [(i, i ^ distance) for i in range(groups)])

    def relay(x):
        turns = [(i, (i + 2 - 4 * (i % 2)) % groups) for i in range(groups)]
        return lax.ppermute(x, both, turns)

    def ring(x):
        turns = [(order[i], order[(i + 1) % ranks]) for i in range(ranks)]
        return lax.ppermute(x, "head", turns)

    capacity = 2 * text_count // groups
    slots = groups // 2 * capacity
    sds = jax.ShapeDtypeStruct
    sk, sv, valid = call(
        functools.partial(slot_kernel, capacity),
        "slots",
        (sds((slots, width), BF),) * 2 + (sds((slots, HD), F32),),
        1,
        (place, text_owner.reshape(1, text_count), text_keys, text_values),
    )
    start_a, late_grad = together(grad_output[:TILE], grad_output)
    part_a, part_b = [start_a], [late_grad[TILE:]]
    mate_v, mate_k, mate_q = swap(values), swap(keys), swap(queries)
    part_a.append(ring(part_a[0]))
    part_b.append(ring(part_b[0]))
    for step in range(ranks - 2):
        if step == ranks - 3:
            first = call(
                first_kernel,
                "first_blocks",
                sds((frame, width), F32),
                1,
                (place, *part_a[:-1], *part_b[:-1], out_weight),
            )
            part_a[-1], mate_v = together(part_a[-1], mate_v)
            part_b[-1], mate_k, first = together(part_b[-1], mate_k, first)
        part_a.append(ring(part_a[-1]))
        part_b.append(ring(part_b[-1]))
    far_v, far_k = relay(mate_v), relay(mate_k)

    second = call(
        functools.partial(second_kernel, ranks - 2),
        "second_blocks",
        sds((frame, width), F32),
        1,
        (place, part_a[-2], part_b[-2], out_weight, first),
    )
    grad_a, grad_b = (
        call(
            functools.partial(last_kernel, ranks - 1, chunk),
            f"grad_heads_{chunk}",
            sds((TILE, width), BF),
            1,
            (place, part, out_weight, second),
        )
        for chunk, part in enumerate((part_a[-1], part_b[-1]))
    )
    late_a, mate_q = together(grad_a, mate_q)
    mate_a, mate_b = swap(late_a), swap(grad_b)
    far_q = relay(mate_q)
    far_k, sk, mate_a = together(far_k, sk, mate_a)
    wide = pltpu.VMEM((3 * frame, width), BF)
    aux, dscores = call(
        softmax_kernel,
        "softmax",
        (sds((2 * AUX, width), BF), sds((2 * (3 * TILE + text_count), width), BF)),
        2,
        (
            place, lists, queries, keys, mate_k, far_k, values, mate_v, far_v,
            text_keys, text_values, grad_a, grad_b,
        ),
        (wide, wide),
    )
    late_aux, mate_b = together(aux, mate_b)
    mate_aux = swap(late_aux)
    own_aux = aux
    acc = sds((frame, width), F32)
    text_acc = sds((slots, width), F32)
    accs = call(
        own_kernel,
        "own_keys",
        (acc, acc, text_acc, text_acc),
        2,
        (place, lists, keys, values, sk, sv, queries, grad_a, grad_b, own_aux),
    )
    key_acc, value_acc, text_k, text_v = accs
    mate_aux, far_q = together(mate_aux, far_q)
    far_a = relay(mate_a)
    mate_aux, far_a = together(mate_aux, far_a)
    keep, send, message = call(
        text_kernel,
        "text_slots",
        (
            sds((slots // 2, 2 * width), F32),
            sds((slots // 2, 2 * width), BF),
            sds((TILE + 2 * AUX, width), BF),
        ),
        0,
        (sk, sv, valid, mate_q, mate_a, mate_b, mate_aux, text_k, text_v),
    )
    far_message = relay(message)
    key_acc, value_acc = call(
        mate_kernel,
        "mate_keys",
        (acc, acc),
        2,
        (place, lists, keys, values, mate_q, mate_a, mate_b, mate_aux, key_acc, value_acc),
    )
    query_grads = call(
        query_kernel,
        "query_grads",
        sds((frame, width), BF),
        2,
        (place, lists, keys, mate_k, far_k, text_keys, dscores),
        (wide,),
    )
    key_grads, value_grads = call(
        far_kernel,
        "far_keys",
        (sds((frame, width), BF),) * 2,
        2,
        (place, lists, keys, values, far_q, far_a, far_message, key_acc, value_acc),
    )
    stages = []
    distance = 2
    while distance < groups:
        stages.append(distance)
        distance *= 2
    for i, d in enumerate(stages):
        arrived = swap(send, d)
        rows = keep.shape[0] // 2
        if i + 1 < len(stages):
            keep, send = call(
                add_kernel,
                f"add_slots_{i}",
                (sds((rows, 2 * width), F32), sds((rows, 2 * width), BF)),
                0,
                (keep, arrived),
            )
    text_key_grads, text_value_grads = call(
        finish_kernel, "finish_slots", (sds((2 * rows, width), BF),) * 2, 0, (keep, arrived)
    )
    return query_grads, key_grads, value_grads, text_key_grads, text_value_grads


def solution(mesh):
    rows = P(("seq", "rep"), "head")
    return jax.shard_map(
        local,
        mesh=mesh,
        in_specs=(rows, rows, rows, rows, P("head", None), P(None, "head"), P(None, "head"), P(), P()),
        out_specs=(rows,) * 5,
        check_vma=False,
    )
```

```python
import functools
import math

import jax
import jax.numpy as jnp
from jax import lax
from jax.experimental import pallas as pl
from jax.experimental.pallas import tpu as pltpu
from jax.sharding import PartitionSpec as P

HD = 128
TILE = 128
AUX = 16
SCALE = HD ** (-0.5)
SCALE2 = SCALE * math.log2(math.e)
OFF = 1e30
GROUP = 3
PAIRS = 3
BF = jnp.bfloat16
F32 = jnp.float32
LIMIT = 16 << 20


def nt(a, b):
    return lax.dot_general(a, b, (((1,), (1,)), ((), ())), preferred_element_type=F32)


def nn(a, b):
    return lax.dot_general(a, b, (((1,), (0,)), ((), ())), preferred_element_type=F32)


def tn(a, b):
    return lax.dot_general(a, b, (((0,), (0,)), ((), ())), preferred_element_type=F32)


def lanes(h):
    return slice(h * HD, (h + 1) * HD)


def source_tile(place, lists, tile, entry):
    slab, mate = place[0], place[1]
    listed = lists[entry, tile]
    owner = lax.shift_right_logical(listed, 1)
    source = jnp.where(owner == slab, 0, jnp.where(owner == mate, 1, 2))
    return pl.multiple_of((source * 2 + (listed & 1)) * TILE, TILE)


def stack_tiles(parts, wide):
    frame = parts[0].shape[0]
    for i, part in enumerate(parts):
        wide[i * frame : (i + 1) * frame, :] = part[...]


def slot_kernel(capacity, place, owner, tk, tv, sk, sv, valid):
    count = owner.shape[1]
    slots = sk.shape[0]
    across = jnp.broadcast_to(owner[...], (count, count))
    down = across.astype(F32).T.astype(jnp.int32)
    line = lax.broadcasted_iota(jnp.int32, (count, count), 0)
    lane = lax.broadcasted_iota(jnp.int32, (count, count), 1)
    rank = jnp.sum(
        jnp.where((across == down) & (line < lane), 1, 0), axis=0, keepdims=True
    )
    slot = owner[...] * capacity + rank
    row = lax.broadcasted_iota(jnp.int32, (slots, count), 0)
    group, inside = row // capacity, row % capacity
    bits = (slots // capacity).bit_length() - 1
    offset = jnp.zeros_like(row)
    for bit in range(bits):
        offset = offset + (((group >> (bits - 1 - bit)) & 1) << (bit + 1))
    wanted = (place[0] ^ offset) * capacity + inside
    chosen = jnp.where(wanted == jnp.broadcast_to(slot, (slots, count)), 1.0, 0.0)
    live = jnp.sum(chosen, axis=1, keepdims=True)
    chosen = chosen.astype(BF)
    sk[...] = nn(chosen, tk[...]).astype(BF)
    sv[...] = nn(chosen, tv[...]).astype(BF)
    valid[...] = jnp.broadcast_to(live, valid.shape)


def gathered(wide, text, starts, cols):
    return jnp.concatenate(
        [wide[pl.ds(a, TILE), cols] for a in starts] + [text[:, cols]], axis=0
    )


def split(x, count):
    parts = []
    for _ in range(count):
        head = x.astype(BF).astype(F32)
        parts.append(head)
        x = x - head
    return parts


def block_of(place, weight, depth, step):
    ranks = weight.shape[1] // depth
    source = place[4 + lax.rem(place[2] - step + ranks, ranks)]
    return weight[:, pl.ds(pl.multiple_of(source * depth, 128), depth)]


def first_kernel(place, *refs):
    n = len(refs) // 2 - 1
    weight, out = refs[2 * n :]
    depth = refs[0].shape[1]
    for chunk in range(2):
        total = None
        for step in range(n):
            term = nt(refs[chunk * n + step][...], block_of(place, weight, depth, step))
            total = term if total is None else total + term
        out[chunk * TILE : (chunk + 1) * TILE, :] = total


def second_kernel(step, place, a_before, b_before, weight, first, out):
    block = block_of(place, weight, a_before.shape[1], step)
    for chunk, part in enumerate((a_before, b_before)):
        rows = slice(chunk * TILE, (chunk + 1) * TILE)
        out[rows, :] = first[rows, :] + nt(part[...], block)


def last_kernel(step, chunk, place, last, weight, second, out):
    block = block_of(place, weight, last.shape[1], step)
    rows = slice(chunk * TILE, (chunk + 1) * TILE)
    out[...] = (second[rows, :] + nt(last[...], block)).astype(BF)


def softmax_kernel(
    place, lists, q, k0, k1, k2, v0, v1, v2, tk, tv, ga, gb, aux, dscores, wide_k, wide_v
):
    stack_tiles((k0, k1, k2), wide_k)
    stack_tiles((v0, v1, v2), wide_v)
    row = lax.broadcasted_iota(jnp.int32, (AUX, TILE), 0)
    size = dscores.shape[0] // 2
    jobs = []
    for tile in range(2):
        starts = [source_tile(place, lists, place[0] * 2 + tile, e) for e in range(3)]
        rows = slice(tile * TILE, (tile + 1) * TILE)
        jobs += [(tile, rows, starts, lanes(h)) for h in range(q.shape[1] // HD)]
    for first in range(0, len(jobs), PAIRS):
        group = jobs[first : first + PAIRS]
        scores = [nt(gathered(wide_k, tk, at, cols), q[rows, cols]) for _, rows, at, cols in group]
        dprobs = [nt(gathered(wide_v, tv, at, cols), (ga, gb)[tile][:, cols]) for tile, _, at, cols in group]
        for (tile, _, _, cols), score, dprob in zip(group, scores, dprobs):
            top = jnp.max(score, axis=0, keepdims=True)
            weight = jnp.exp2((score - top) * SCALE2)
            total = jnp.sum(weight, axis=0, keepdims=True)
            prob = weight * (1.0 / total)
            delta = jnp.sum(prob * dprob, axis=0, keepdims=True)
            dscores[tile * size : (tile + 1) * size, cols] = (prob * (dprob - delta)).astype(BF)
            lse = top * SCALE2 + jnp.log2(total)
            block = jnp.zeros((AUX, TILE), F32)
            for i, line in enumerate(split(delta, 2) + split(lse, 3)):
                block = jnp.where(row == i, jnp.broadcast_to(line, (AUX, TILE)), block)
            aux[tile * AUX : (tile + 1) * AUX, cols] = block.astype(BF)


def query_kernel(place, lists, k0, k1, k2, tk, dscores, out, wide_k):
    stack_tiles((k0, k1, k2), wide_k)
    size = dscores.shape[0] // 2
    for tile in range(2):
        starts = [source_tile(place, lists, place[0] * 2 + tile, e) for e in range(3)]
        rows = slice(tile * TILE, (tile + 1) * TILE)
        for h in range(out.shape[1] // HD):
            cols = lanes(h)
            dscore = dscores[tile * size : (tile + 1) * size, cols]
            keys = gathered(wide_k, tk, starts, cols)
            out[rows, cols] = (SCALE * tn(dscore, keys)).astype(BF)


def read_lines(aux, chunk, cols):
    lines = aux[chunk * AUX : (chunk + 1) * AUX, cols].astype(F32)
    return lines[0:1] + lines[1:2], (lines[2:3] + lines[3:4]) + lines[4:5]


def off_by(place, lists, slab, tile, key_tile):
    count = lists.shape[1]
    query_tile = slab * 2 + tile
    row = jnp.clip(query_tile, 0, count - 1)
    wanted = place[0] * 2 + key_tile
    found = (lists[0, row] == wanted) | (lists[1, row] == wanted) | (lists[2, row] == wanted)
    found = found & (query_tile >= 0) & (query_tile < count)
    return jnp.where(found, 0.0, OFF)


def key_terms(offs, keys, values, q, ga, gb, aux, emit):
    heads = [lanes(h) for h in range(q.shape[1] // HD)]
    for first in range(0, len(heads), GROUP):
        group = heads[first : first + GROUP]
        q_rows = [q[:, cols] for cols in group]
        g_rows = [jnp.concatenate([ga[:, cols], gb[:, cols]], axis=0) for cols in group]
        scores = [nt(keys(cols), rows) for cols, rows in zip(group, q_rows)]
        dprobs = [nt(values(cols), rows) for cols, rows in zip(group, g_rows)]
        probs, dscores = [], []
        for cols, score, dprob in zip(group, scores, dprobs):
            lines = [read_lines(aux, i, cols) for i in range(2)]
            delta = jnp.concatenate([d for d, _ in lines], axis=1)
            lse = [l for _, l in lines]
            score = score * SCALE2
            pieces = []
            if offs is not None:
                for i in range(2):
                    line = jnp.concatenate([lse[t] + offs[t][i] for t in range(2)], axis=1)
                    pieces.append(score[i * TILE : (i + 1) * TILE] - line)
            done = len(pieces) * TILE
            if score.shape[0] > done:
                pieces.append(score[done:] - jnp.concatenate(lse, axis=1))
            prob = jnp.exp2(jnp.concatenate(pieces, axis=0))
            probs.append(prob.astype(BF))
            dscores.append((prob * (dprob - delta)).astype(BF))
        sums_k = [nn(dscore, rows) for dscore, rows in zip(dscores, q_rows)]
        sums_v = [nn(prob, rows) for prob, rows in zip(probs, g_rows)]
        for cols, dk, dv in zip(group, sums_k, sums_v):
            emit(cols, dk, dv)


def all_offs(place, lists, slab):
    return [[off_by(place, lists, slab, t, i) for i in range(2)] for t in range(2)]


def whole(ref):
    return lambda cols: ref[:, cols]


def own_kernel(sk, sv, q, ga, gb, aux, text_k, text_v):
    def emit(cols, dk, dv):
        text_k[:, cols] = dk
        text_v[:, cols] = dv

    key_terms(None, whole(sk), whole(sv), q, ga, gb, aux, emit)


def text_kernel(sk, sv, valid, q, ga, gb, aux, text_k, text_v, keep, send, message):
    width = q.shape[1]
    half = keep.shape[0]
    live = valid[...] > 0
    message[:TILE, :] = gb[...]
    message[TILE:, :] = aux[...]

    def emit(cols, dk, dv):
        more = slice(cols.start + width, cols.stop + width)
        part_k = jnp.where(live, (text_k[:, cols] + dk) * SCALE, 0.0)
        part_v = jnp.where(live, text_v[:, cols] + dv, 0.0)
        keep[:, cols] = part_k[:half]
        keep[:, more] = part_v[:half]
        send[:, cols] = part_k[half:].astype(BF)
        send[:, more] = part_v[half:].astype(BF)

    key_terms(None, whole(sk), whole(sv), q, ga, gb, aux, emit)


def near_kernel(
    place, lists, k, v, q0, ga0, gb0, aux0, q1, ga1, gb1, aux1, key_acc, value_acc
):
    def put(cols, dk, dv):
        key_acc[:, cols] = dk
        value_acc[:, cols] = dv

    def add(cols, dk, dv):
        key_acc[:, cols] = key_acc[:, cols] + dk
        value_acc[:, cols] = value_acc[:, cols] + dv

    key_terms(all_offs(place, lists, place[0]), whole(k), whole(v), q0, ga0, gb0, aux0, put)
    key_terms(all_offs(place, lists, place[1]), whole(k), whole(v), q1, ga1, gb1, aux1, add)


def far_kernel(place, lists, k, v, q, ga, message, key_acc, value_acc, key_out, value_out):
    gb, aux = message.at[:TILE], message.at[TILE:]

    def emit(cols, dk, dv):
        key_out[:, cols] = ((key_acc[:, cols] + dk) * SCALE).astype(BF)
        value_out[:, cols] = (value_acc[:, cols] + dv).astype(BF)

    key_terms(all_offs(place, lists, place[3]), whole(k), whole(v), q, ga, gb, aux, emit)


def add_kernel(keep, arrived, more, send):
    rows = more.shape[0]
    more[...] = keep[:rows, :] + arrived[:rows, :].astype(F32)
    send[...] = (keep[rows:, :] + arrived[rows:, :].astype(F32)).astype(BF)


def finish_kernel(keep, arrived, key_out, value_out):
    width = key_out.shape[1]
    total = (keep[...] + arrived[...].astype(F32)).astype(BF)
    key_out[...] = total[:, :width]
    value_out[...] = total[:, width:]


VMEM = pl.BlockSpec(memory_space=pltpu.VMEM)
SMEM = pl.BlockSpec(memory_space=pltpu.SMEM)


def call(kernel, name, outs, scalars, arrays, scratch=()):
    return pl.pallas_call(
        kernel,
        name=name,
        out_shape=outs,
        in_specs=[SMEM] * scalars + [VMEM] * (len(arrays) - scalars),
        out_specs=jax.tree.map(lambda _: VMEM, outs),
        scratch_shapes=list(scratch),
        compiler_params=pltpu.CompilerParams(vmem_limit_bytes=LIMIT),
    )(*arrays)


def together(*arrays):
    return lax.optimization_barrier(arrays)


def local(
    queries, keys, values, grad_output, out_weight, text_keys, text_values, mask_lists, text_owner
):
    frame, width = queries.shape
    text_count = text_keys.shape[0]
    both = ("seq", "rep")
    seqs, reps, ranks = lax.axis_size("seq"), lax.axis_size("rep"), lax.axis_size("head")
    groups = seqs * reps
    lists = mask_lists.T
    slab = lax.axis_index(both)
    mate = slab ^ 1
    other = jnp.where(slab & 1, slab + 1, slab - 1)
    order = list(range(0, ranks, 2)) + list(range(1, ranks, 2))[::-1]
    seat = sum(
        jnp.where(lax.axis_index("head") == rank, i, 0) for i, rank in enumerate(order)
    )
    place = jnp.stack([slab, mate, seat, other, *order]).astype(jnp.int32)

    def swap(x, distance=1):
        return lax.ppermute(x, both, [(i, i ^ distance) for i in range(groups)])

    def relay(x):
        turns = [(i, (i + 2 - 4 * (i % 2)) % groups) for i in range(groups)]
        return lax.ppermute(x, both, turns)

    def ring(x):
        turns = [(order[i], order[(i + 1) % ranks]) for i in range(ranks)]
        return lax.ppermute(x, "head", turns)

    capacity = 2 * text_count // groups
    slots = groups // 2 * capacity
    sds = jax.ShapeDtypeStruct
    sk, sv, valid = call(
        functools.partial(slot_kernel, capacity),
        "slots",
        (sds((slots, width), BF),) * 2 + (sds((slots, HD), F32),),
        1,
        (place, text_owner.reshape(1, text_count), text_keys, text_values),
    )
    start_a, late_grad = together(grad_output[:TILE], grad_output)
    part_a, part_b = [start_a], [late_grad[TILE:]]
    mate_v, mate_k, mate_q = swap(values), swap(keys), swap(queries)
    part_a.append(ring(part_a[0]))
    part_b.append(ring(part_b[0]))
    for step in range(ranks - 2):
        if step == ranks - 3:
            first = call(
                first_kernel,
                "first_blocks",
                sds((frame, width), F32),
                1,
                (place, *part_a[:-1], *part_b[:-1], out_weight),
            )
            part_a[-1], mate_v = together(part_a[-1], mate_v)
            part_b[-1], mate_k, first = together(part_b[-1], mate_k, first)
        part_a.append(ring(part_a[-1]))
        part_b.append(ring(part_b[-1]))
    far_v, far_k = relay(mate_v), relay(mate_k)

    second = call(
        functools.partial(second_kernel, ranks - 2),
        "second_blocks",
        sds((frame, width), F32),
        1,
        (place, part_a[-2], part_b[-2], out_weight, first),
    )
    grad_a, grad_b = (
        call(
            functools.partial(last_kernel, ranks - 1, chunk),
            f"grad_heads_{chunk}",
            sds((TILE, width), BF),
            1,
            (place, part, out_weight, second),
        )
        for chunk, part in enumerate((part_a[-1], part_b[-1]))
    )
    late_a, mate_q = together(grad_a, mate_q)
    mate_a, mate_b = swap(late_a), swap(grad_b)
    far_q = relay(mate_q)
    far_k, mate_a = together(far_k, mate_a)
    wide = pltpu.VMEM((3 * frame, width), BF)
    aux, dscores = call(
        softmax_kernel,
        "softmax",
        (sds((2 * AUX, width), BF), sds((2 * (3 * TILE + text_count), width), BF)),
        2,
        (
            place, lists, queries, keys, mate_k, far_k, values, mate_v, far_v,
            text_keys, text_values, grad_a, grad_b,
        ),
        (wide, wide),
    )
    late_aux, mate_b = together(aux, mate_b)
    mate_aux = swap(late_aux)
    own_aux = aux
    acc = sds((frame, width), F32)
    text_acc = sds((slots, width), F32)
    text_k, text_v = call(
        own_kernel,
        "own_slots",
        (text_acc, text_acc),
        0,
        (sk, sv, queries, grad_a, grad_b, own_aux),
    )
    mate_aux, far_q = together(mate_aux, far_q)
    far_a = relay(mate_a)
    mate_aux, far_a = together(mate_aux, far_a)
    keep, send, message = call(
        text_kernel,
        "text_slots",
        (
            sds((slots // 2, 2 * width), F32),
            sds((slots // 2, 2 * width), BF),
            sds((TILE + 2 * AUX, width), BF),
        ),
        0,
        (sk, sv, valid, mate_q, mate_a, mate_b, mate_aux, text_k, text_v),
    )
    far_message = relay(message)
    key_acc, value_acc = call(
        near_kernel,
        "near_keys",
        (acc, acc),
        2,
        (
            place, lists, keys, values, queries, grad_a, grad_b, own_aux,
            mate_q, mate_a, mate_b, mate_aux,
        ),
    )
    query_grads = call(
        query_kernel,
        "query_grads",
        sds((frame, width), BF),
        2,
        (place, lists, keys, mate_k, far_k, text_keys, dscores),
        (wide,),
    )
    key_grads, value_grads = call(
        far_kernel,
        "far_keys",
        (sds((frame, width), BF),) * 2,
        2,
        (place, lists, keys, values, far_q, far_a, far_message, key_acc, value_acc),
    )
    stages = []
    distance = 2
    while distance < groups:
        stages.append(distance)
        distance *= 2
    for i, d in enumerate(stages):
        arrived = swap(send, d)
        rows = keep.shape[0] // 2
        if i + 1 < len(stages):
            keep, send = call(
                add_kernel,
                f"add_slots_{i}",
                (sds((rows, 2 * width), F32), sds((rows, 2 * width), BF)),
                0,
                (keep, arrived),
            )
    text_key_grads, text_value_grads = call(
        finish_kernel, "finish_slots", (sds((2 * rows, width), BF),) * 2, 0, (keep, arrived)
    )
    return query_grads, key_grads, value_grads, text_key_grads, text_value_grads


def solution(mesh):
    rows = P(("seq", "rep"), "head")
    return jax.shard_map(
        local,
        mesh=mesh,
        in_specs=(rows, rows, rows, rows, P("head", None), P(None, "head"), P(None, "head"), P(), P()),
        out_specs=(rows,) * 5,
        check_vma=False,
    )
```

```python
import functools
import math

import jax
import jax.numpy as jnp
from jax import lax
from jax.experimental import pallas as pl
from jax.experimental.pallas import tpu as pltpu
from jax.sharding import PartitionSpec as P

HD = 128
TILE = 128
AUX = 16
SCALE = HD ** (-0.5)
SCALE2 = SCALE * math.log2(math.e)
OFF = 1e30
GROUP = 3
PAIRS = 3
BF = jnp.bfloat16
F32 = jnp.float32
LIMIT = 16 << 20


def nt(a, b):
    return lax.dot_general(a, b, (((1,), (1,)), ((), ())), preferred_element_type=F32)


def nn(a, b):
    return lax.dot_general(a, b, (((1,), (0,)), ((), ())), preferred_element_type=F32)


def tn(a, b):
    return lax.dot_general(a, b, (((0,), (0,)), ((), ())), preferred_element_type=F32)


def lanes(h):
    return slice(h * HD, (h + 1) * HD)


def source_tile(place, lists, tile, entry):
    slab, mate = place[0], place[1]
    listed = lists[entry, tile]
    owner = lax.shift_right_logical(listed, 1)
    source = jnp.where(owner == slab, 0, jnp.where(owner == mate, 1, 2))
    return pl.multiple_of((source * 2 + (listed & 1)) * TILE, TILE)


def stack_tiles(parts, wide):
    frame = parts[0].shape[0]
    for i, part in enumerate(parts):
        wide[i * frame : (i + 1) * frame, :] = part[...]


def slot_kernel(capacity, place, owner, tk, tv, sk, sv, valid):
    count = owner.shape[1]
    slots = sk.shape[0]
    across = jnp.broadcast_to(owner[...], (count, count))
    down = across.astype(F32).T.astype(jnp.int32)
    line = lax.broadcasted_iota(jnp.int32, (count, count), 0)
    lane = lax.broadcasted_iota(jnp.int32, (count, count), 1)
    rank = jnp.sum(
        jnp.where((across == down) & (line < lane), 1, 0), axis=0, keepdims=True
    )
    slot = owner[...] * capacity + rank
    row = lax.broadcasted_iota(jnp.int32, (slots, count), 0)
    group, inside = row // capacity, row % capacity
    bits = (slots // capacity).bit_length() - 1
    offset = jnp.zeros_like(row)
    for bit in range(bits):
        offset = offset + (((group >> (bits - 1 - bit)) & 1) << (bit + 1))
    wanted = (place[0] ^ offset) * capacity + inside
    chosen = jnp.where(wanted == jnp.broadcast_to(slot, (slots, count)), 1.0, 0.0)
    live = jnp.sum(chosen, axis=1, keepdims=True)
    chosen = chosen.astype(BF)
    sk[...] = nn(chosen, tk[...]).astype(BF)
    sv[...] = nn(chosen, tv[...]).astype(BF)
    valid[...] = jnp.broadcast_to(live, valid.shape)


def gathered(wide, text, starts, cols):
    return jnp.concatenate(
        [wide[pl.ds(a, TILE), cols] for a in starts] + [text[:, cols]], axis=0
    )


def split(x, count):
    parts = []
    for _ in range(count):
        head = x.astype(BF).astype(F32)
        parts.append(head)
        x = x - head
    return parts


def block_of(place, weight, depth, step):
    ranks = weight.shape[1] // depth
    source = place[4 + lax.rem(place[2] - step + ranks, ranks)]
    return weight[:, pl.ds(pl.multiple_of(source * depth, 128), depth)]


def first_kernel(place, *refs):
    n = len(refs) // 2 - 1
    weight, out = refs[2 * n :]
    depth = refs[0].shape[1]
    for chunk in range(2):
        total = None
        for step in range(n):
            term = nt(refs[chunk * n + step][...], block_of(place, weight, depth, step))
            total = term if total is None else total + term
        out[chunk * TILE : (chunk + 1) * TILE, :] = total


def second_kernel(step, place, a_before, b_before, weight, first, out):
    block = block_of(place, weight, a_before.shape[1], step)
    for chunk, part in enumerate((a_before, b_before)):
        rows = slice(chunk * TILE, (chunk + 1) * TILE)
        out[rows, :] = first[rows, :] + nt(part[...], block)


def last_kernel(step, chunk, place, last, weight, second, out):
    block = block_of(place, weight, last.shape[1], step)
    rows = slice(chunk * TILE, (chunk + 1) * TILE)
    out[...] = (second[rows, :] + nt(last[...], block)).astype(BF)


def softmax_kernel(
    place, lists, q, k0, k1, k2, v0, v1, v2, tk, tv, ga, gb, aux, dscores, wide_k, wide_v
):
    stack_tiles((k0, k1, k2), wide_k)
    stack_tiles((v0, v1, v2), wide_v)
    row = lax.broadcasted_iota(jnp.int32, (AUX, TILE), 0)
    size = dscores.shape[0] // 2
    jobs = []
    for tile in range(2):
        starts = [source_tile(place, lists, place[0] * 2 + tile, e) for e in range(3)]
        rows = slice(tile * TILE, (tile + 1) * TILE)
        jobs += [(tile, rows, starts, lanes(h)) for h in range(q.shape[1] // HD)]
    for first in range(0, len(jobs), PAIRS):
        group = jobs[first : first + PAIRS]
        scores = [nt(gathered(wide_k, tk, at, cols), q[rows, cols]) for _, rows, at, cols in group]
        dprobs = [nt(gathered(wide_v, tv, at, cols), (ga, gb)[tile][:, cols]) for tile, _, at, cols in group]
        for (tile, _, _, cols), score, dprob in zip(group, scores, dprobs):
            top = jnp.max(score, axis=0, keepdims=True)
            weight = jnp.exp2((score - top) * SCALE2)
            total = jnp.sum(weight, axis=0, keepdims=True)
            prob = weight * (1.0 / total)
            delta = jnp.sum(prob * dprob, axis=0, keepdims=True)
            dscores[tile * size : (tile + 1) * size, cols] = (prob * (dprob - delta)).astype(BF)
            lse = top * SCALE2 + jnp.log2(total)
            block = jnp.zeros((AUX, TILE), F32)
            for i, line in enumerate(split(delta, 2) + split(lse, 3)):
                block = jnp.where(row == i, jnp.broadcast_to(line, (AUX, TILE)), block)
            aux[tile * AUX : (tile + 1) * AUX, cols] = block.astype(BF)


def query_kernel(place, lists, k0, k1, k2, tk, dscores, out, wide_k):
    stack_tiles((k0, k1, k2), wide_k)
    size = dscores.shape[0] // 2
    for tile in range(2):
        starts = [source_tile(place, lists, place[0] * 2 + tile, e) for e in range(3)]
        rows = slice(tile * TILE, (tile + 1) * TILE)
        for h in range(out.shape[1] // HD):
            cols = lanes(h)
            dscore = dscores[tile * size : (tile + 1) * size, cols]
            keys = gathered(wide_k, tk, starts, cols)
            out[rows, cols] = (SCALE * tn(dscore, keys)).astype(BF)


def read_lines(aux, chunk, cols):
    lines = aux[chunk * AUX : (chunk + 1) * AUX, cols].astype(F32)
    return lines[0:1] + lines[1:2], (lines[2:3] + lines[3:4]) + lines[4:5]


def off_by(place, lists, slab, tile, key_tile):
    count = lists.shape[1]
    query_tile = slab * 2 + tile
    row = jnp.clip(query_tile, 0, count - 1)
    wanted = place[0] * 2 + key_tile
    found = (lists[0, row] == wanted) | (lists[1, row] == wanted) | (lists[2, row] == wanted)
    found = found & (query_tile >= 0) & (query_tile < count)
    return jnp.where(found, 0.0, OFF)


def key_terms(offs, keys, values, q, ga, gb, aux, emit):
    heads = [lanes(h) for h in range(q.shape[1] // HD)]
    for first in range(0, len(heads), GROUP):
        group = heads[first : first + GROUP]
        q_rows = [q[:, cols] for cols in group]
        g_rows = [jnp.concatenate([ga[:, cols], gb[:, cols]], axis=0) for cols in group]
        scores = [nt(keys(cols), rows) for cols, rows in zip(group, q_rows)]
        dprobs = [nt(values(cols), rows) for cols, rows in zip(group, g_rows)]
        probs, dscores = [], []
        for cols, score, dprob in zip(group, scores, dprobs):
            lines = [read_lines(aux, i, cols) for i in range(2)]
            delta = jnp.concatenate([d for d, _ in lines], axis=1)
            lse = [l for _, l in lines]
            score = score * SCALE2
            pieces = []
            if offs is not None:
                for i in range(2):
                    line = jnp.concatenate([lse[t] + offs[t][i] for t in range(2)], axis=1)
                    pieces.append(score[i * TILE : (i + 1) * TILE] - line)
            done = len(pieces) * TILE
            if score.shape[0] > done:
                pieces.append(score[done:] - jnp.concatenate(lse, axis=1))
            prob = jnp.exp2(jnp.concatenate(pieces, axis=0))
            probs.append(prob.astype(BF))
            dscores.append((prob * (dprob - delta)).astype(BF))
        sums_k = [nn(dscore, rows) for dscore, rows in zip(dscores, q_rows)]
        sums_v = [nn(prob, rows) for prob, rows in zip(probs, g_rows)]
        for cols, dk, dv in zip(group, sums_k, sums_v):
            emit(cols, dk, dv)


def all_offs(place, lists, slab):
    return [[off_by(place, lists, slab, t, i) for i in range(2)] for t in range(2)]


def whole(ref):
    return lambda cols: ref[:, cols]


def own_kernel(sk, sv, q, ga, gb, aux, text_k, text_v):
    def emit(cols, dk, dv):
        text_k[:, cols] = dk
        text_v[:, cols] = dv

    key_terms(None, whole(sk), whole(sv), q, ga, gb, aux, emit)


def text_kernel(sk, sv, valid, q, ga, gb, aux, text_k, text_v, keep, send, message):
    width = q.shape[1]
    half = keep.shape[0]
    live = valid[...] > 0
    message[:TILE, :] = gb[...]
    message[TILE:, :] = aux[...]

    def emit(cols, dk, dv):
        more = slice(cols.start + width, cols.stop + width)
        part_k = jnp.where(live, (text_k[:, cols] + dk) * SCALE, 0.0)
        part_v = jnp.where(live, text_v[:, cols] + dv, 0.0)
        keep[:, cols] = part_k[:half]
        keep[:, more] = part_v[:half]
        send[:, cols] = part_k[half:].astype(BF)
        send[:, more] = part_v[half:].astype(BF)

    key_terms(None, whole(sk), whole(sv), q, ga, gb, aux, emit)


def near_kernel(
    place, lists, k, v, q0, ga0, gb0, aux0, q1, ga1, gb1, aux1, key_acc, value_acc
):
    def put(cols, dk, dv):
        key_acc[:, cols] = dk
        value_acc[:, cols] = dv

    def add(cols, dk, dv):
        key_acc[:, cols] = key_acc[:, cols] + dk
        value_acc[:, cols] = value_acc[:, cols] + dv

    key_terms(all_offs(place, lists, place[0]), whole(k), whole(v), q0, ga0, gb0, aux0, put)
    key_terms(all_offs(place, lists, place[1]), whole(k), whole(v), q1, ga1, gb1, aux1, add)


def query_near_kernel(
    place, lists, k, v, q0, ga0, gb0, aux0, q1, ga1, gb1, aux1, k1, k2, tk, dscores,
    out, key_acc, value_acc, wide_k, buf, sem,
):
    query_kernel(place, lists, k, k1, k2, tk, dscores, buf, wide_k)
    copy = pltpu.make_async_copy(buf, out, sem)
    copy.start()
    near_kernel(
        place, lists, k, v, q0, ga0, gb0, aux0, q1, ga1, gb1, aux1, key_acc, value_acc
    )
    copy.wait()


def far_kernel(place, lists, k, v, q, ga, message, key_acc, value_acc, key_out, value_out):
    gb, aux = message.at[:TILE], message.at[TILE:]

    def emit(cols, dk, dv):
        key_out[:, cols] = ((key_acc[:, cols] + dk) * SCALE).astype(BF)
        value_out[:, cols] = (value_acc[:, cols] + dv).astype(BF)

    key_terms(all_offs(place, lists, place[3]), whole(k), whole(v), q, ga, gb, aux, emit)


def add_kernel(keep, arrived, more, send):
    rows = more.shape[0]
    more[...] = keep[:rows, :] + arrived[:rows, :].astype(F32)
    send[...] = (keep[rows:, :] + arrived[rows:, :].astype(F32)).astype(BF)


def finish_kernel(keep, arrived, key_out, value_out):
    width = key_out.shape[1]
    total = (keep[...] + arrived[...].astype(F32)).astype(BF)
    key_out[...] = total[:, :width]
    value_out[...] = total[:, width:]


VMEM = pl.BlockSpec(memory_space=pltpu.VMEM)
SMEM = pl.BlockSpec(memory_space=pltpu.SMEM)


def call(kernel, name, outs, scalars, arrays, scratch=(), out_specs=None):
    return pl.pallas_call(
        kernel,
        name=name,
        out_shape=outs,
        in_specs=[SMEM] * scalars + [VMEM] * (len(arrays) - scalars),
        out_specs=out_specs or jax.tree.map(lambda _: VMEM, outs),
        scratch_shapes=list(scratch),
        compiler_params=pltpu.CompilerParams(vmem_limit_bytes=LIMIT),
    )(*arrays)


def together(*arrays):
    return lax.optimization_barrier(arrays)


def local(
    queries, keys, values, grad_output, out_weight, text_keys, text_values, mask_lists, text_owner
):
    frame, width = queries.shape
    text_count = text_keys.shape[0]
    both = ("seq", "rep")
    seqs, reps, ranks = lax.axis_size("seq"), lax.axis_size("rep"), lax.axis_size("head")
    groups = seqs * reps
    lists = mask_lists.T
    slab = lax.axis_index(both)
    mate = slab ^ 1
    other = jnp.where(slab & 1, slab + 1, slab - 1)
    order = list(range(0, ranks, 2)) + list(range(1, ranks, 2))[::-1]
    seat = sum(
        jnp.where(lax.axis_index("head") == rank, i, 0) for i, rank in enumerate(order)
    )
    place = jnp.stack([slab, mate, seat, other, *order]).astype(jnp.int32)

    def swap(x, distance=1):
        return lax.ppermute(x, both, [(i, i ^ distance) for i in range(groups)])

    def relay(x):
        turns = [(i, (i + 2 - 4 * (i % 2)) % groups) for i in range(groups)]
        return lax.ppermute(x, both, turns)

    def ring(x):
        turns = [(order[i], order[(i + 1) % ranks]) for i in range(ranks)]
        return lax.ppermute(x, "head", turns)

    capacity = 2 * text_count // groups
    slots = groups // 2 * capacity
    sds = jax.ShapeDtypeStruct
    sk, sv, valid = call(
        functools.partial(slot_kernel, capacity),
        "slots",
        (sds((slots, width), BF),) * 2 + (sds((slots, HD), F32),),
        1,
        (place, text_owner.reshape(1, text_count), text_keys, text_values),
    )
    start_a, late_grad = together(grad_output[:TILE], grad_output)
    part_a, part_b = [start_a], [late_grad[TILE:]]
    mate_v, mate_k, mate_q = swap(values), swap(keys), swap(queries)
    part_a.append(ring(part_a[0]))
    part_b.append(ring(part_b[0]))
    for step in range(ranks - 2):
        if step == ranks - 3:
            first = call(
                first_kernel,
                "first_blocks",
                sds((frame, width), F32),
                1,
                (place, *part_a[:-1], *part_b[:-1], out_weight),
            )
            part_a[-1], mate_v = together(part_a[-1], mate_v)
            part_b[-1], mate_k, first = together(part_b[-1], mate_k, first)
        part_a.append(ring(part_a[-1]))
        part_b.append(ring(part_b[-1]))
    far_v, far_k = relay(mate_v), relay(mate_k)

    second = call(
        functools.partial(second_kernel, ranks - 2),
        "second_blocks",
        sds((frame, width), F32),
        1,
        (place, part_a[-2], part_b[-2], out_weight, first),
    )
    grad_a, grad_b = (
        call(
            functools.partial(last_kernel, ranks - 1, chunk),
            f"grad_heads_{chunk}",
            sds((TILE, width), BF),
            1,
            (place, part, out_weight, second),
        )
        for chunk, part in enumerate((part_a[-1], part_b[-1]))
    )
    late_a, mate_q = together(grad_a, mate_q)
    mate_a, mate_b = swap(late_a), swap(grad_b)
    far_q = relay(mate_q)
    far_k, mate_a = together(far_k, mate_a)
    wide = pltpu.VMEM((3 * frame, width), BF)
    aux, dscores = call(
        softmax_kernel,
        "softmax",
        (sds((2 * AUX, width), BF), sds((2 * (3 * TILE + text_count), width), BF)),
        2,
        (
            place, lists, queries, keys, mate_k, far_k, values, mate_v, far_v,
            text_keys, text_values, grad_a, grad_b,
        ),
        (wide, wide),
    )
    late_aux, mate_b = together(aux, mate_b)
    mate_aux = swap(late_aux)
    own_aux = aux
    acc = sds((frame, width), F32)
    text_acc = sds((slots, width), F32)
    text_k, text_v = call(
        own_kernel,
        "own_slots",
        (text_acc, text_acc),
        0,
        (sk, sv, queries, grad_a, grad_b, own_aux),
    )
    mate_aux, far_q = together(mate_aux, far_q)
    far_a = relay(mate_a)
    mate_aux, far_a = together(mate_aux, far_a)
    keep, send, message = call(
        text_kernel,
        "text_slots",
        (
            sds((slots // 2, 2 * width), F32),
            sds((slots // 2, 2 * width), BF),
            sds((TILE + 2 * AUX, width), BF),
        ),
        0,
        (sk, sv, valid, mate_q, mate_a, mate_b, mate_aux, text_k, text_v),
    )
    far_message = relay(message)
    query_grads, key_acc, value_acc = call(
        query_near_kernel,
        "query_near_keys",
        (sds((frame, width), BF), acc, acc),
        2,
        (
            place, lists, keys, values, queries, grad_a, grad_b, own_aux,
            mate_q, mate_a, mate_b, mate_aux, mate_k, far_k, text_keys, dscores,
        ),
        (wide, pltpu.VMEM((frame, width), BF), pltpu.SemaphoreType.DMA),
        (pl.BlockSpec(memory_space=pl.ANY), VMEM, VMEM),
    )
    key_grads, value_grads = call(
        far_kernel,
        "far_keys",
        (sds((frame, width), BF),) * 2,
        2,
        (place, lists, keys, values, far_q, far_a, far_message, key_acc, value_acc),
    )
    stages = []
    distance = 2
    while distance < groups:
        stages.append(distance)
        distance *= 2
    for i, d in enumerate(stages):
        arrived = swap(send, d)
        rows = keep.shape[0] // 2
        if i + 1 < len(stages):
            keep, send = call(
                add_kernel,
                f"add_slots_{i}",
                (sds((rows, 2 * width), F32), sds((rows, 2 * width), BF)),
                0,
                (keep, arrived),
            )
    text_key_grads, text_value_grads = call(
        finish_kernel, "finish_slots", (sds((2 * rows, width), BF),) * 2, 0, (keep, arrived)
    )
    return query_grads, key_grads, value_grads, text_key_grads, text_value_grads


def solution(mesh):
    rows = P(("seq", "rep"), "head")
    return jax.shard_map(
        local,
        mesh=mesh,
        in_specs=(rows, rows, rows, rows, P("head", None), P(None, "head"), P(None, "head"), P(), P()),
        out_specs=(rows,) * 5,
        check_vma=False,
    )
```

```python
import functools
import math

import jax
import jax.numpy as jnp
from jax import lax
from jax.experimental import pallas as pl
from jax.experimental.pallas import tpu as pltpu
from jax.sharding import PartitionSpec as P

HD = 128
TILE = 128
AUX = 16
SCALE = HD ** (-0.5)
SCALE2 = SCALE * math.log2(math.e)
OFF = 1e30
GROUP = 3
PAIRS = 3
BF = jnp.bfloat16
F32 = jnp.float32
LIMIT = 16 << 20


def nt(a, b):
    return lax.dot_general(a, b, (((1,), (1,)), ((), ())), preferred_element_type=F32)


def nn(a, b):
    return lax.dot_general(a, b, (((1,), (0,)), ((), ())), preferred_element_type=F32)


def tn(a, b):
    return lax.dot_general(a, b, (((0,), (0,)), ((), ())), preferred_element_type=F32)


def lanes(h):
    return slice(h * HD, (h + 1) * HD)


def source_tile(place, lists, tile, entry):
    slab, mate = place[0], place[1]
    listed = lists[entry, tile]
    owner = lax.shift_right_logical(listed, 1)
    source = jnp.where(owner == slab, 0, jnp.where(owner == mate, 1, 2))
    return pl.multiple_of((source * 2 + (listed & 1)) * TILE, TILE)


def stack_tiles(parts, wide):
    frame = parts[0].shape[0]
    for i, part in enumerate(parts):
        wide[i * frame : (i + 1) * frame, :] = part[...]


def slot_kernel(capacity, place, owner, tk, tv, sk, sv, valid):
    count = owner.shape[1]
    slots = sk.shape[0]
    across = jnp.broadcast_to(owner[...], (count, count))
    down = across.astype(F32).T.astype(jnp.int32)
    line = lax.broadcasted_iota(jnp.int32, (count, count), 0)
    lane = lax.broadcasted_iota(jnp.int32, (count, count), 1)
    rank = jnp.sum(
        jnp.where((across == down) & (line < lane), 1, 0), axis=0, keepdims=True
    )
    slot = owner[...] * capacity + rank
    row = lax.broadcasted_iota(jnp.int32, (slots, count), 0)
    group, inside = row // capacity, row % capacity
    bits = (slots // capacity).bit_length() - 1
    offset = jnp.zeros_like(row)
    for bit in range(bits):
        offset = offset + (((group >> (bits - 1 - bit)) & 1) << (bit + 1))
    wanted = (place[0] ^ offset) * capacity + inside
    chosen = jnp.where(wanted == jnp.broadcast_to(slot, (slots, count)), 1.0, 0.0)
    live = jnp.sum(chosen, axis=1, keepdims=True)
    chosen = chosen.astype(BF)
    sk[...] = nn(chosen, tk[...]).astype(BF)
    sv[...] = nn(chosen, tv[...]).astype(BF)
    valid[...] = jnp.broadcast_to(live, valid.shape)


def gathered(wide, text, starts, cols):
    return jnp.concatenate(
        [wide[pl.ds(a, TILE), cols] for a in starts] + [text[:, cols]], axis=0
    )


def split(x, count):
    parts = []
    for _ in range(count):
        head = x.astype(BF).astype(F32)
        parts.append(head)
        x = x - head
    return parts


def block_of(place, weight, depth, step):
    ranks = weight.shape[1] // depth
    source = place[4 + lax.rem(place[2] - step + ranks, ranks)]
    return weight[:, pl.ds(pl.multiple_of(source * depth, 128), depth)]


def first_kernel(place, *refs):
    n = len(refs) // 2 - 1
    weight, out = refs[2 * n :]
    depth = refs[0].shape[1]
    for chunk in range(2):
        total = None
        for step in range(n):
            term = nt(refs[chunk * n + step][...], block_of(place, weight, depth, step))
            total = term if total is None else total + term
        out[chunk * TILE : (chunk + 1) * TILE, :] = total


def second_kernel(step, place, a_before, b_before, weight, first, out):
    block = block_of(place, weight, a_before.shape[1], step)
    for chunk, part in enumerate((a_before, b_before)):
        rows = slice(chunk * TILE, (chunk + 1) * TILE)
        out[rows, :] = first[rows, :] + nt(part[...], block)


def last_kernel(step, chunk, place, last, weight, second, out):
    block = block_of(place, weight, last.shape[1], step)
    rows = slice(chunk * TILE, (chunk + 1) * TILE)
    out[...] = (second[rows, :] + nt(last[...], block)).astype(BF)


def softmax_kernel(
    place, lists, q, k0, k1, k2, v0, v1, v2, tk, tv, ga, gb, aux, dscores, wide_k, wide_v
):
    stack_tiles((k0, k1, k2), wide_k)
    stack_tiles((v0, v1, v2), wide_v)
    row = lax.broadcasted_iota(jnp.int32, (AUX, TILE), 0)
    size = dscores.shape[0] // 2
    jobs = []
    for tile in range(2):
        starts = [source_tile(place, lists, place[0] * 2 + tile, e) for e in range(3)]
        rows = slice(tile * TILE, (tile + 1) * TILE)
        jobs += [(tile, rows, starts, lanes(h)) for h in range(q.shape[1] // HD)]
    for first in range(0, len(jobs), PAIRS):
        group = jobs[first : first + PAIRS]
        scores = [nt(gathered(wide_k, tk, at, cols), q[rows, cols]) for _, rows, at, cols in group]
        dprobs = [nt(gathered(wide_v, tv, at, cols), (ga, gb)[tile][:, cols]) for tile, _, at, cols in group]
        for (tile, _, _, cols), score, dprob in zip(group, scores, dprobs):
            top = jnp.max(score, axis=0, keepdims=True)
            weight = jnp.exp2((score - top) * SCALE2)
            total = jnp.sum(weight, axis=0, keepdims=True)
            prob = weight * (1.0 / total)
            delta = jnp.sum(prob * dprob, axis=0, keepdims=True)
            dscores[tile * size : (tile + 1) * size, cols] = (prob * (dprob - delta)).astype(BF)
            lse = top * SCALE2 + jnp.log2(total)
            block = jnp.zeros((AUX, TILE), F32)
            for i, line in enumerate(split(delta, 2) + split(lse, 3)):
                block = jnp.where(row == i, jnp.broadcast_to(line, (AUX, TILE)), block)
            aux[tile * AUX : (tile + 1) * AUX, cols] = block.astype(BF)


def query_kernel(place, lists, k0, k1, k2, tk, dscores, out, wide_k):
    stack_tiles((k0, k1, k2), wide_k)
    size = dscores.shape[0] // 2
    for tile in range(2):
        starts = [source_tile(place, lists, place[0] * 2 + tile, e) for e in range(3)]
        rows = slice(tile * TILE, (tile + 1) * TILE)
        for h in range(out.shape[1] // HD):
            cols = lanes(h)
            dscore = dscores[tile * size : (tile + 1) * size, cols]
            keys = gathered(wide_k, tk, starts, cols)
            out[rows, cols] = (SCALE * tn(dscore, keys)).astype(BF)


def read_lines(aux, chunk, cols):
    lines = aux[chunk * AUX : (chunk + 1) * AUX, cols].astype(F32)
    return lines[0:1] + lines[1:2], (lines[2:3] + lines[3:4]) + lines[4:5]


def off_by(place, lists, slab, tile, key_tile):
    count = lists.shape[1]
    query_tile = slab * 2 + tile
    row = jnp.clip(query_tile, 0, count - 1)
    wanted = place[0] * 2 + key_tile
    found = (lists[0, row] == wanted) | (lists[1, row] == wanted) | (lists[2, row] == wanted)
    found = found & (query_tile >= 0) & (query_tile < count)
    return jnp.where(found, 0.0, OFF)


def key_terms(offs, keys, values, q, ga, gb, aux, emit):
    heads = [lanes(h) for h in range(q.shape[1] // HD)]
    for first in range(0, len(heads), GROUP):
        group = heads[first : first + GROUP]
        q_rows = [q[:, cols] for cols in group]
        g_rows = [jnp.concatenate([ga[:, cols], gb[:, cols]], axis=0) for cols in group]
        scores = [nt(keys(cols), rows) for cols, rows in zip(group, q_rows)]
        dprobs = [nt(values(cols), rows) for cols, rows in zip(group, g_rows)]
        probs, dscores = [], []
        for cols, score, dprob in zip(group, scores, dprobs):
            lines = [read_lines(aux, i, cols) for i in range(2)]
            delta = jnp.concatenate([d for d, _ in lines], axis=1)
            lse = [l for _, l in lines]
            score = score * SCALE2
            pieces = []
            if offs is not None:
                for i in range(2):
                    line = jnp.concatenate([lse[t] + offs[t][i] for t in range(2)], axis=1)
                    pieces.append(score[i * TILE : (i + 1) * TILE] - line)
            done = len(pieces) * TILE
            if score.shape[0] > done:
                pieces.append(score[done:] - jnp.concatenate(lse, axis=1))
            prob = jnp.exp2(jnp.concatenate(pieces, axis=0))
            probs.append(prob.astype(BF))
            dscores.append((prob * (dprob - delta)).astype(BF))
        sums_k = [nn(dscore, rows) for dscore, rows in zip(dscores, q_rows)]
        sums_v = [nn(prob, rows) for prob, rows in zip(probs, g_rows)]
        for cols, dk, dv in zip(group, sums_k, sums_v):
            emit(cols, dk, dv)


def all_offs(place, lists, slab):
    return [[off_by(place, lists, slab, t, i) for i in range(2)] for t in range(2)]


def whole(ref):
    return lambda cols: ref[:, cols]


def own_kernel(sk, sv, q, ga, gb, aux, text_k, text_v):
    def emit(cols, dk, dv):
        text_k[:, cols] = dk
        text_v[:, cols] = dv

    key_terms(None, whole(sk), whole(sv), q, ga, gb, aux, emit)


def text_kernel(sk, sv, valid, q, ga, gb, aux, text_k, text_v, keep, send, message):
    width = q.shape[1]
    half = keep.shape[0]
    live = valid[...] > 0
    message[:TILE, :] = gb[...]
    message[TILE:, :] = aux[...]

    def emit(cols, dk, dv):
        more = slice(cols.start + width, cols.stop + width)
        part_k = jnp.where(live, (text_k[:, cols] + dk) * SCALE, 0.0)
        part_v = jnp.where(live, text_v[:, cols] + dv, 0.0)
        keep[:, cols] = part_k[:half]
        keep[:, more] = part_v[:half]
        send[:, cols] = part_k[half:].astype(BF)
        send[:, more] = part_v[half:].astype(BF)

    key_terms(None, whole(sk), whole(sv), q, ga, gb, aux, emit)


def near_kernel(
    place, lists, k, v, q0, ga0, gb0, aux0, q1, ga1, gb1, aux1, key_acc, value_acc
):
    def put(cols, dk, dv):
        key_acc[:, cols] = dk
        value_acc[:, cols] = dv

    def add(cols, dk, dv):
        key_acc[:, cols] = key_acc[:, cols] + dk
        value_acc[:, cols] = value_acc[:, cols] + dv

    key_terms(all_offs(place, lists, place[0]), whole(k), whole(v), q0, ga0, gb0, aux0, put)
    key_terms(all_offs(place, lists, place[1]), whole(k), whole(v), q1, ga1, gb1, aux1, add)


def query_near_kernel(
    place, lists, k, v, q0, ga0, gb0, aux0, q1, ga1, gb1, aux1, k1, k2, tk, dscores,
    out, key_acc, value_acc, wide_k, buf, sem,
):
    query_kernel(place, lists, k, k1, k2, tk, dscores, buf, wide_k)
    copy = pltpu.make_async_copy(buf, out, sem)
    copy.start()
    near_kernel(
        place, lists, k, v, q0, ga0, gb0, aux0, q1, ga1, gb1, aux1, key_acc, value_acc
    )
    copy.wait()


def far_kernel(place, lists, k, v, q, ga, message, key_acc, value_acc, key_out, value_out):
    gb, aux = message.at[:TILE], message.at[TILE:]

    def emit(cols, dk, dv):
        key_out[:, cols] = ((key_acc[:, cols] + dk) * SCALE).astype(BF)
        value_out[:, cols] = (value_acc[:, cols] + dv).astype(BF)

    key_terms(all_offs(place, lists, place[3]), whole(k), whole(v), q, ga, gb, aux, emit)


def add_kernel(keep, arrived, more, send):
    rows = more.shape[0]
    more[...] = keep[:rows, :] + arrived[:rows, :].astype(F32)
    send[...] = (keep[rows:, :] + arrived[rows:, :].astype(F32)).astype(BF)


def finish_kernel(keep, arrived, key_out, value_out):
    width = key_out.shape[1]
    total = (keep[...] + arrived[...].astype(F32)).astype(BF)
    key_out[...] = total[:, :width]
    value_out[...] = total[:, width:]


VMEM = pl.BlockSpec(memory_space=pltpu.VMEM)
SMEM = pl.BlockSpec(memory_space=pltpu.SMEM)


def call(kernel, name, outs, scalars, arrays, scratch=(), out_specs=None):
    return pl.pallas_call(
        kernel,
        name=name,
        out_shape=outs,
        in_specs=[SMEM] * scalars + [VMEM] * (len(arrays) - scalars),
        out_specs=out_specs or jax.tree.map(lambda _: VMEM, outs),
        scratch_shapes=list(scratch),
        compiler_params=pltpu.CompilerParams(vmem_limit_bytes=LIMIT),
    )(*arrays)


def together(*arrays):
    return lax.optimization_barrier(arrays)


def local(
    queries, keys, values, grad_output, out_weight, text_keys, text_values, mask_lists, text_owner
):
    frame, width = queries.shape
    text_count = text_keys.shape[0]
    both = ("seq", "rep")
    seqs, reps, ranks = lax.axis_size("seq"), lax.axis_size("rep"), lax.axis_size("head")
    groups = seqs * reps
    lists = mask_lists.T
    slab = lax.axis_index(both)
    mate = slab ^ 1
    other = jnp.where(slab & 1, slab + 1, slab - 1)
    order = list(range(0, ranks, 2)) + list(range(1, ranks, 2))[::-1]
    seat = sum(
        jnp.where(lax.axis_index("head") == rank, i, 0) for i, rank in enumerate(order)
    )
    place = jnp.stack([slab, mate, seat, other, *order]).astype(jnp.int32)

    def swap(x, distance=1):
        return lax.ppermute(x, both, [(i, i ^ distance) for i in range(groups)])

    def relay(x):
        turns = [(i, (i + 2 - 4 * (i % 2)) % groups) for i in range(groups)]
        return lax.ppermute(x, both, turns)

    def ring(x):
        turns = [(order[i], order[(i + 1) % ranks]) for i in range(ranks)]
        return lax.ppermute(x, "head", turns)

    capacity = 2 * text_count // groups
    slots = groups // 2 * capacity
    sds = jax.ShapeDtypeStruct
    sk, sv, valid = call(
        functools.partial(slot_kernel, capacity),
        "slots",
        (sds((slots, width), BF),) * 2 + (sds((slots, HD), F32),),
        1,
        (place, text_owner.reshape(1, text_count), text_keys, text_values),
    )
    start_a, late_grad = together(grad_output[:TILE], grad_output)
    part_a, part_b = [start_a], [late_grad[TILE:]]
    mate_v, mate_k, mate_q = swap(values), swap(keys), swap(queries)
    part_a.append(ring(part_a[0]))
    part_b.append(ring(part_b[0]))
    for step in range(ranks - 2):
        if step == ranks - 3:
            first = call(
                first_kernel,
                "first_blocks",
                sds((frame, width), F32),
                1,
                (place, *part_a[:-1], *part_b[:-1], out_weight),
            )
            part_a[-1], mate_v = together(part_a[-1], mate_v)
            part_b[-1], mate_k, first = together(part_b[-1], mate_k, first)
        part_a.append(ring(part_a[-1]))
        part_b.append(ring(part_b[-1]))
    far_v, far_k = relay(mate_v), relay(mate_k)

    second = call(
        functools.partial(second_kernel, ranks - 2),
        "second_blocks",
        sds((frame, width), F32),
        1,
        (place, part_a[-2], part_b[-2], out_weight, first),
    )
    grad_a, grad_b = (
        call(
            functools.partial(last_kernel, ranks - 1, chunk),
            f"grad_heads_{chunk}",
            sds((TILE, width), BF),
            1,
            (place, part, out_weight, second),
        )
        for chunk, part in enumerate((part_a[-1], part_b[-1]))
    )
    late_a, mate_q = together(grad_a, mate_q)
    mate_a, mate_b = swap(late_a), swap(grad_b)
    far_q = relay(mate_q)
    far_k, mate_a = together(far_k, mate_a)
    wide = pltpu.VMEM((3 * frame, width), BF)
    aux, dscores = call(
        softmax_kernel,
        "softmax",
        (sds((2 * AUX, width), BF), sds((2 * (3 * TILE + text_count), width), BF)),
        2,
        (
            place, lists, queries, keys, mate_k, far_k, values, mate_v, far_v,
            text_keys, text_values, grad_a, grad_b,
        ),
        (wide, wide),
    )
    late_aux, mate_b = together(aux, mate_b)
    mate_aux = swap(late_aux)
    own_aux = aux
    acc = sds((frame, width), F32)
    text_acc = sds((slots, width), F32)
    text_k, text_v = call(
        own_kernel,
        "own_slots",
        (text_acc, text_acc),
        0,
        (sk, sv, queries, grad_a, grad_b, own_aux),
    )
    mate_aux, far_q = together(mate_aux, far_q)
    mate_a, sk = together(mate_a, sk)
    far_a = relay(mate_a)
    mate_aux, far_a = together(mate_aux, far_a)
    keep, send, message = call(
        text_kernel,
        "text_slots",
        (
            sds((slots // 2, 2 * width), F32),
            sds((slots // 2, 2 * width), BF),
            sds((TILE + 2 * AUX, width), BF),
        ),
        0,
        (sk, sv, valid, mate_q, mate_a, mate_b, mate_aux, text_k, text_v),
    )
    far_message = relay(message)
    query_grads, key_acc, value_acc = call(
        query_near_kernel,
        "query_near_keys",
        (sds((frame, width), BF), acc, acc),
        2,
        (
            place, lists, keys, values, queries, grad_a, grad_b, own_aux,
            mate_q, mate_a, mate_b, mate_aux, mate_k, far_k, text_keys, dscores,
        ),
        (wide, pltpu.VMEM((frame, width), BF), pltpu.SemaphoreType.DMA),
        (pl.BlockSpec(memory_space=pl.ANY), VMEM, VMEM),
    )
    key_grads, value_grads = call(
        far_kernel,
        "far_keys",
        (sds((frame, width), BF),) * 2,
        2,
        (place, lists, keys, values, far_q, far_a, far_message, key_acc, value_acc),
    )
    stages = []
    distance = 2
    while distance < groups:
        stages.append(distance)
        distance *= 2
    for i, d in enumerate(stages):
        arrived = swap(send, d)
        rows = keep.shape[0] // 2
        if i + 1 < len(stages):
            keep, send = call(
                add_kernel,
                f"add_slots_{i}",
                (sds((rows, 2 * width), F32), sds((rows, 2 * width), BF)),
                0,
                (keep, arrived),
            )
    text_key_grads, text_value_grads = call(
        finish_kernel, "finish_slots", (sds((2 * rows, width), BF),) * 2, 0, (keep, arrived)
    )
    return query_grads, key_grads, value_grads, text_key_grads, text_value_grads


def solution(mesh):
    rows = P(("seq", "rep"), "head")
    return jax.shard_map(
        local,
        mesh=mesh,
        in_specs=(rows, rows, rows, rows, P("head", None), P(None, "head"), P(None, "head"), P(), P()),
        out_specs=(rows,) * 5,
        check_vma=False,
    )
```
